1024 devices in a mesh: exp: 64 (over x_lo, z), dp: 16 (over x_hi, y, core).
Axes of the slice: x: 4 (x_hi: 2, x_lo: 2; x = x_hi * 2 + x_lo), y: 4, z: 32, core: 2. Of those that a mesh axis runs over, the one named last changes fastest.
Arguments:
- hidden_acts: bfloat16 [64, 2048, 1024], P('exp', 'dp'), may hold values from -6 to 6
- train_rows: int32 [64, 2048], P('exp', 'dp'), may hold values from 0 to 255
- out_grad: bfloat16 [4096, 3584], P('dp'), may hold values from -0.1796875 to 0.1796875
- master: float32 [64, 1024, 3584], P('exp', 'dp'), may hold values from -0.1875 to 0.1875
- moment1: bfloat16 [64, 1024, 3584], P('exp', 'dp'), may hold values from -0.119628906 to 0.119628906
- moment2: bfloat16 [64, 1024, 3584], P('exp', 'dp'), may hold values from 0.0049743652 to 0.049804688
- gate_up: bfloat16 [64, 3584, 2, 1024], P('exp', 'dp'), may hold values from -0.09375 to 0.09375
- dec_tokens: bfloat16 [512, 3584], P('exp', 'dp'), may hold values from -6 to 6
- route_ids: int32 [512, 8], P('exp'), may hold values from 0 to 63, all different within a row; in each aligned block of 8 rows (0 to 7, 8 to 15, ...) at most 2 rows name the same one
- route_gates: float32 [512, 8], P('exp'), may hold values from 0.1 to 1
Outputs:
- moe_out: bfloat16 [512, 3584], P('exp', 'dp')
The draws below stay inside these ranges and needn't reach their ends.
Inputs may be any that keep to these rules, and one draw needn't show every extreme that they name: `route_ids`: each row names 8 different experts; among the 8 rows of one index of exp no expert is named more than 2 times, a bound that some block reaches.
All inputs are finite; a program needn't handle non-finite values.
Results may differ from the reference program's by a relative error of at most 0.03.
Values may be sent and summed in bfloat16 or wider, within the bound.
No kernel may reach another device: no remote copies, remote signals or barrier semaphores. Data moves between devices by JAX's collectives and lax.ppermute only.
A program may use at most 64 MiB of HBM per device.

```python
import math
import jax
import jax.numpy as jnp
import numpy as np
from jax import lax

D = 3584
F = 1024
TK = 128
TTOK = 256
DTOK = 8
TOPK = 8
EXPERTS = 64
CAP = 2
SLOTS = 128
DSHARD = 224
N_EXP = 64
N_DP = 16


def place_ends(values, rng, low, top_value):
    index_at = [jax.random.randint(jax.random.fold_in(rng, axis), (), 0, length) for axis, length in enumerate(values.shape)]
    main_axis = values.shape.index(max(values.shape))
    neighbour = index_at[:main_axis] + [(index_at[main_axis] + 1) % values.shape[main_axis]] + index_at[main_axis + 1:]
    return values.at[tuple(index_at)].set(low).at[tuple(neighbour)].set(top_value)


def block_levels(own_key, shape, shards, low, largest):
    gain, own = 1.0, jax.random.fold_in(own_key, 6)
    for dim, blocks in shards:
        steps = jnp.exp(jax.random.uniform(jax.random.fold_in(own, dim), (blocks,), jnp.float32, low / len(shards), largest / len(shards)))
        gain = gain * jnp.repeat(steps, shape[dim] // blocks).reshape([-1 if axis == dim else 1 for axis in range(len(shape))])
    return gain


def assign_block(own_key, own, number, rows, number_of, top, bound, lean):
    sequence = jax.random.permutation(own_key, number_of)
    heavy_load, ordinary = shares(number_of, rows * top, bound, lean, True), shares(number_of, rows * top, bound, lean, False)
    places = jnp.arange(number_of)

    def named(tallies, offset_by):
        used = int((tallies > 0).sum())
        fixed = max(1, used // 4)
        shifted = fixed + (places - fixed + offset_by * (used - fixed)) % max(1, number_of - fixed)
        return jnp.zeros((number_of,), jnp.int32).at[sequence[jnp.where(places < fixed, places, shifted)]].set(jnp.asarray(tallies, jnp.int32))

    tallies = jnp.where(number % 4 == 0, named(heavy_load, number // 4), named(ordinary, number - number // 4 - 1))
    mixed = jax.random.permutation(jax.random.fold_in(own, 3), number_of)
    donor, sink = mixed[0:number_of // 2 * 2:2], mixed[1:number_of // 2 * 2:2]
    slack = jnp.minimum(tallies[donor] - 1, bound - tallies[sink]) // 2
    slack = jnp.where((donor == sequence[0]) | (sink == sequence[0]) | (tallies[sink] == 0), 0, jnp.maximum(slack, 0))
    shifted = jax.random.randint(jax.random.fold_in(own, 4), (number_of // 2,), 0, 1 << 20) % (slack + 1)
    tallies = tallies.at[donor].add(-shifted).at[sink].add(shifted)
    members = jnp.searchsorted(jnp.cumsum(tallies), jnp.arange(rows * top), side="right").astype(jnp.int32)
    table = members.reshape(top, rows).T
    table = table[jax.random.permutation(jax.random.fold_in(own, 1), rows)]
    offset_by = jax.random.randint(jax.random.fold_in(own, 2), (rows, 1), 0, top)
    return jnp.take_along_axis(table, (jnp.arange(top)[None, :] + offset_by) % top, axis=1)


def shares(amount, total, limit, lean, full):
    weights = [(1 << 20) // math.isqrt(grade ** lean) + 1 for grade in range(1, amount + 1)]
    largest = limit if full else min(limit, max(-(-total // amount), total * weights[0] // sum(weights)))
    least = 1 if total - largest >= amount - 1 else 0
    holding, surplus = [largest] + [least] * (amount - 1), total - largest - least * (amount - 1)
    while surplus > 0:
        free = [i for i in range(1, amount) if holding[i] < largest] or [i for i in range(1, amount) if holding[i] < limit]
        pool, remaining = sum([weights[i] for i in free]), surplus
        for i in free:
            extra = min(limit - holding[i], max(1, remaining * weights[i] // pool), surplus)
            holding[i] = holding[i] + extra
            surplus = surplus - extra
    return np.array(holding)


def centred(own_key, dims, width, reach, pieces=(), held_as=jnp.bfloat16):
    factor_of = block_levels(own_key, dims, pieces, -0.22, 0.18) if pieces else 1.0
    values = jax.random.normal(own_key, dims, jnp.float32) * width * factor_of
    return jnp.minimum(jnp.maximum(values, -reach), reach).astype(held_as)


def setup_inputs(seed: int = 0) -> dict:
    key_of = jax.random.split(jax.random.key(seed), 11)
    hidden_acts = centred(key_of[0], (EXPERTS, N_DP * TK, F), 1.0, 6.0, ((0, 64), (1, 16)))
    train_rows = place_ends(jax.random.randint(key_of[1], (EXPERTS, N_DP * TK), 0, TTOK), jax.random.fold_in(key_of[1], 1), 0, TTOK - 1).astype(jnp.int32)
    out_grad = centred(key_of[2], (N_DP * TTOK, D), 0.03, 0.1796875, ((0, 16),))
    master = centred(key_of[3], (EXPERTS, F, D), F ** -0.5, 0.1875, ((0, 64), (1, 16)), jnp.float32)
    moment1 = centred(key_of[4], (EXPERTS, F, D), 0.02, 0.119628906, ((0, 64), (1, 16)))
    moment2 = jnp.clip(jnp.exp(math.log(0.049804688) - 2.3038113 * jax.random.uniform(key_of[5], (EXPERTS, F, D), jnp.float32) ** block_levels(key_of[5], (EXPERTS, F, D), ((0, 64), (1, 16)), -0.2, 0.2)), 0.0049743652, 0.049804688).astype(jnp.bfloat16)
    gate_up = centred(key_of[6], (EXPERTS, D, 2, F), D ** -0.5, 0.09375, ((0, 64), (1, 16)))
    dec_tokens = centred(key_of[7], (N_EXP * DTOK, D), 1.0, 6.0, ((0, 64), (1, 16)))
    route_ids_keys = jax.random.split(jax.random.fold_in(key_of[8], 1), (N_EXP * DTOK) // DTOK)
    route_ids_turns = jax.random.permutation(jax.random.fold_in(key_of[8], 3), (N_EXP * DTOK) // DTOK)
    route_ids = jax.vmap(lambda own, number: assign_block(jax.random.fold_in(key_of[8], 2), own, number, DTOK, EXPERTS, TOPK, CAP, 2))(route_ids_keys, route_ids_turns).reshape((N_EXP * DTOK, TOPK))
    route_gates = jnp.clip(jnp.exp(math.log(1.0) - 2.3025851 * jax.random.uniform(key_of[9], (N_EXP * DTOK, TOPK), jnp.float32) ** block_levels(key_of[9], (N_EXP * DTOK, TOPK), ((0, 64),), -0.2, 0.2)), 0.1, 1.0)
    return {"hidden_acts": hidden_acts, "train_rows": train_rows, "out_grad": out_grad, "master": master, "moment1": moment1, "moment2": moment2, "gate_up": gate_up, "dec_tokens": dec_tokens, "route_ids": route_ids, "route_gates": route_gates}


beta_one = 0.9
beta_two = 0.95
learn_rate = 0.1
weight_decay = 0.1
epsilon = 1e-08
bias_first = 1.0 - 0.9 ** 20
bias_second = 1.0 - 0.95 ** 20

def round_trip(values):
    return lax.optimization_barrier(values.astype(jnp.bfloat16)).astype(jnp.float32)

def slot_table(route_ids):
    blocked = route_ids.reshape(N_EXP, DTOK * TOPK)
    onehot = (blocked[:, :, None] == jnp.arange(EXPERTS, dtype=jnp.int32)[None, None, :]).astype(jnp.int32)
    earlier = jnp.cumsum(onehot, axis=1) - onehot
    position = lax.optimization_barrier(jnp.sum(earlier * onehot, axis=2))
    slot_index = blocked * CAP + position
    return (slot_index[:, :, None] == jnp.arange(SLOTS, dtype=jnp.int32)[None, None, :]).astype(jnp.float32)

def reference(hidden_acts, train_rows, out_grad, master, moment1, moment2, gate_up, dec_tokens, route_ids, route_gates):
    placement = slot_table(route_ids)
    repeated = jnp.repeat(dec_tokens.reshape(N_EXP, DTOK, D), TOPK, axis=1).astype(jnp.float32)
    outgoing = jnp.einsum('ors,ord->osd', placement, repeated).astype(jnp.bfloat16)
    arriving = outgoing.reshape(N_EXP, EXPERTS, CAP, D).transpose(1, 0, 2, 3).reshape(EXPERTS, SLOTS, D)
    activations = hidden_acts.reshape(EXPERTS, N_DP, TK, F)
    rows_all = train_rows.reshape(EXPERTS, N_DP, TK)
    cotangent = out_grad.reshape(N_DP, TTOK, D)

    def one_expert(items):
        acts_e, rows_e, master_e, first_e, second_e, gate_e, arrived = items
        selected = jax.vmap(lambda table, index: table[index])(cotangent, rows_e)
        product = jnp.einsum('ntf,ntd->nfd', acts_e.astype(jnp.float32), selected.astype(jnp.float32))
        gradient = lax.optimization_barrier(jnp.sum(round_trip(product), axis=0))
        first = beta_one * first_e.astype(jnp.float32) + (1.0 - beta_one) * gradient
        second = beta_two * second_e.astype(jnp.float32) + (1.0 - beta_two) * gradient * gradient
        update = first / bias_first / (jnp.sqrt(second / bias_second) + epsilon)
        down_tile = (master_e * (1.0 - learn_rate * weight_decay) - learn_rate * update).astype(jnp.bfloat16)
        blocks = jnp.einsum('snd,ndgf->nsgf', arrived.reshape(SLOTS, N_DP, DSHARD).astype(jnp.float32), gate_e.reshape(N_DP, DSHARD, 2, F).astype(jnp.float32))
        mixed = lax.optimization_barrier(jnp.sum(round_trip(blocks), axis=0))
        hidden = (jax.nn.silu(mixed[:, 0]) * mixed[:, 1]).astype(jnp.bfloat16)
        return jnp.dot(hidden, down_tile, preferred_element_type=jnp.float32).astype(jnp.bfloat16)
    results = lax.map(one_expert, (activations, rows_all, master, moment1, moment2, gate_up, arriving))
    returned = results.reshape(EXPERTS, N_EXP, CAP, D).transpose(1, 0, 2, 3).reshape(N_EXP, SLOTS, D)
    chosen = jnp.einsum('ors,osd->ord', placement, returned.astype(jnp.float32))
    weighted = chosen.reshape(N_EXP * DTOK, TOPK, D) * route_gates[:, :, None]
    return lax.optimization_barrier(jnp.sum(weighted, axis=1)).astype(jnp.bfloat16)
```

```python
import functools

import jax
import jax.numpy as jnp
from jax import lax
from jax.experimental import pallas as pl
from jax.experimental.pallas import tpu as pltpu
from jax.sharding import PartitionSpec as P

beta_one = 0.9
beta_two = 0.95
learn_rate = 0.1
weight_decay = 0.1
epsilon = 1e-08
bias_first = 1.0 - 0.9**20
bias_second = 1.0 - 0.95**20

HALVES, RING, CORES = 2, 4, 2
SMEM = pl.BlockSpec(memory_space=pltpu.SMEM)
LIMIT = 48 * 2**20


def whole(*shape):
    return pl.BlockSpec(shape, lambda *_: (0,) * len(shape))


def contract_first(left, right):
    return lax.dot_general(
        left, right, (((0,), (0,)), ((), ())), preferred_element_type=jnp.float32
    )


def permutation(half_step, ring_step, core_step):
    pairs = []
    for half in range(HALVES):
        for ring in range(RING):
            for core in range(CORES):
                source = (half * RING + ring) * CORES + core
                target = (half ^ half_step) * RING + (ring + ring_step) % RING
                pairs.append((source, target * CORES + (core ^ core_step)))
    return pairs


def pack_kernel(place_ref, rows_ref, grad_ref, master_ref, first_ref, second_ref, *outs):
    table, columns = grad_ref.shape
    tokens = rows_ref.shape[1]
    rows = master_ref.shape[1]
    run = columns // (HALVES * RING)
    onehot = (lax.broadcasted_iota(jnp.int32, (table, tokens), 0) == rows_ref[...]).astype(
        jnp.float32
    ).astype(jnp.bfloat16)
    ring = place_ref[1]
    for here in range(RING):

        @pl.when(ring == here)
        def _(here=here):
            for step in range(RING):
                out = outs[step]
                for half in range(HALVES):
                    start = (half * RING + (here + step) % RING) * run
                    take = pl.ds(start, run)
                    put = pl.ds(half * run, run)
                    out[0:tokens, put] = contract_first(onehot, grad_ref[:, take]).astype(
                        jnp.bfloat16
                    )
                    at = tokens
                    out[at : at + rows, put] = master_ref[0, :, take].astype(jnp.bfloat16)
                    out[at + rows : at + 2 * rows, put] = first_ref[0, :, take]
                    out[at + 2 * rows : at + 3 * rows, put] = second_ref[0, :, take]


def pack(place, train_rows, out_grad, master, moment1, moment2):
    tokens = train_rows.shape[1]
    rows = master.shape[1]
    shape = (tokens + 3 * rows, out_grad.shape[1] // RING)
    return pl.pallas_call(
        pack_kernel,
        out_shape=[jax.ShapeDtypeStruct(shape, jnp.bfloat16)] * RING,
        in_specs=[SMEM] + [pl.BlockSpec(memory_space=pltpu.VMEM)] * 5,
        out_specs=[pl.BlockSpec(memory_space=pltpu.VMEM)] * RING,
        compiler_params=pltpu.CompilerParams(vmem_limit_bytes=LIMIT),
        cost_estimate=pl.CostEstimate(
            flops=2 * tokens * out_grad.size, bytes_accessed=7_000_000, transcendentals=0
        ),
    )(place, train_rows, out_grad, master, moment1, moment2)


def gradient_kernel(place_ref, acts_ref, *refs):
    parts, (theirs_ref, ours_ref) = refs[:RING], refs[RING:]
    ring, core = place_ref[1], place_ref[2]
    acts = [acts_ref[(ring - step + RING) % RING] for step in range(RING)]
    total = None
    for step in range(0, RING, 2):
        left = jnp.concatenate([acts[step], acts[step + 1]], axis=0)
        right = jnp.concatenate([parts[step][...], parts[step + 1][...]], axis=0)
        product = contract_first(left, right)
        total = product if total is None else total + product
    rows = total.shape[0] // 2
    upper, lower = total[:rows], total[rows:]
    ours_ref[0] = jnp.where(core == 0, upper, lower)
    theirs_ref[0] = jnp.where(core == 0, lower, upper).astype(jnp.bfloat16)


def gradients(place, acts, parts):
    ring_tokens, units = acts.shape
    tokens = ring_tokens // RING
    width = parts[0].shape[1]
    blocks = HALVES * RING
    block = units // blocks
    rows = block // 2
    return pl.pallas_call(
        gradient_kernel,
        grid=(blocks,),
        out_shape=[
            jax.ShapeDtypeStruct((blocks, rows, width), jnp.bfloat16),
            jax.ShapeDtypeStruct((blocks, rows, width), jnp.float32),
        ],
        in_specs=[SMEM, pl.BlockSpec((RING, tokens, block), lambda i: (0, 0, i))]
        + [whole(tokens, width)] * RING,
        out_specs=[pl.BlockSpec((1, rows, width), lambda i: (i, 0, 0))] * 2,
        compiler_params=pltpu.CompilerParams(vmem_limit_bytes=LIMIT),
        cost_estimate=pl.CostEstimate(
            flops=2 * units * width * ring_tokens, bytes_accessed=5_000_000, transcendentals=0
        ),
    )(place, acts.reshape(RING, tokens, units), *parts)


def adam_kernel(tokens, place_ref, ours_ref, near_ref, far_ref, *refs):
    states, outs = refs[:RING], refs[RING:]
    half, ring, core = place_ref[0], place_ref[1], place_ref[2]
    rows, columns = far_ref.shape[1:]
    width = columns // len(outs)
    for step in range(RING):
        source = (ring - step + RING) % RING
        block = half * RING + source
        gradient = (
            ours_ref[block]
            + near_ref[block].astype(jnp.float32)
            + far_ref[source].astype(jnp.float32)
        )
        state = states[step]
        master = state[tokens : tokens + rows, :].astype(jnp.float32)
        first_old = state[tokens + rows : tokens + 2 * rows, :].astype(jnp.float32)
        second_old = state[tokens + 2 * rows : tokens + 3 * rows, :].astype(jnp.float32)
        first = beta_one * first_old + (1.0 - beta_one) * gradient
        second = beta_two * second_old + (1.0 - beta_two) * gradient * gradient
        update = first / bias_first / (jnp.sqrt(second / bias_second) + epsilon)
        tile = (master * (1.0 - learn_rate * weight_decay) - learn_rate * update).astype(
            jnp.bfloat16
        )
        put = pl.ds(pl.multiple_of(source * rows, rows), rows)
        for here in range(HALVES * CORES):

            @pl.when(half * CORES + core == here)
            def _(here=here, put=put, tile=tile):
                for block in range(HALVES * CORES):
                    outs[block ^ here][put, :] = tile[:, block * width : (block + 1) * width]


def adam_tiles(tokens, place, ours, near, far, parts):
    rows, columns = far.shape[1:]
    groups = HALVES * CORES
    return pl.pallas_call(
        functools.partial(adam_kernel, tokens),
        out_shape=[jax.ShapeDtypeStruct((RING * rows, columns // groups), jnp.bfloat16)] * groups,
        in_specs=[SMEM] + [pl.BlockSpec(memory_space=pltpu.VMEM)] * (3 + RING),
        out_specs=[pl.BlockSpec(memory_space=pltpu.VMEM)] * groups,
        compiler_params=pltpu.CompilerParams(vmem_limit_bytes=LIMIT),
        cost_estimate=pl.CostEstimate(
            flops=20 * far.size, bytes_accessed=6_500_000, transcendentals=2 * far.size
        ),
    )(place, ours, near, far, *parts)


def results_kernel(place_ref, hidden_ref, *refs):
    tiles, out_ref = refs[:-1], refs[-1]
    half, core = place_ref[0], place_ref[2]
    total = None
    for relative, tile in enumerate(tiles):
        from_half = jnp.bitwise_xor(half, relative // CORES)
        from_core = jnp.bitwise_xor(core, relative % CORES)
        hidden = jnp.concatenate(
            [hidden_ref[(from_half * RING + ring) * CORES + from_core] for ring in range(RING)],
            axis=0,
        )
        product = contract_first(hidden, tile[...])
        total = product if total is None else total + product
    out_ref[...] = total.astype(jnp.bfloat16)


def expert_results(place, hidden, tiles):
    slots, width = hidden.shape[2], tiles[0].shape[1]
    return pl.pallas_call(
        results_kernel,
        out_shape=jax.ShapeDtypeStruct((slots, width), jnp.bfloat16),
        in_specs=[SMEM] + [pl.BlockSpec(memory_space=pltpu.VMEM)] * (1 + len(tiles)),
        out_specs=pl.BlockSpec(memory_space=pltpu.VMEM),
        compiler_params=pltpu.CompilerParams(vmem_limit_bytes=LIMIT),
        cost_estimate=pl.CostEstimate(
            flops=2 * hidden.size * width, bytes_accessed=800_000, transcendentals=0
        ),
    )(place, hidden, *tiles)


def body(
    hidden_acts,
    train_rows,
    out_grad,
    master,
    moment1,
    moment2,
    gate_up,
    dec_tokens,
    route_ids,
    route_gates,
):
    index = lax.axis_index("dp")
    shards = lax.axis_size("dp")
    half, ring, core = index >> 3, (index >> 1) & (RING - 1), index & (CORES - 1)
    place = jnp.stack([half, ring, core]).astype(jnp.int32)
    token_count, width = dec_tokens.shape
    tokens = train_rows.shape[1]

    rings = [
        [(h * RING + r) * CORES + c for r in range(RING)]
        for h in range(HALVES)
        for c in range(CORES)
    ]
    acts = lax.all_gather(hidden_acts[0], "dp", axis=0, tiled=True, axis_index_groups=rings)
    sends = pack(place, train_rows, out_grad, master, moment1, moment2)
    parts = [sends[0]] + [
        lax.ppermute(sends[step], "dp", permutation(0, step, 0)) for step in range(1, RING)
    ]

    choices_per = route_ids.shape[1]
    expert_count = lax.axis_size("exp")
    capacity = min(token_count, max(2, 2 * choices_per * token_count // expert_count))
    slot_count = expert_count * capacity
    flat_ids = route_ids.reshape(-1)
    onehot = (flat_ids[:, None] == jnp.arange(expert_count, dtype=jnp.int32)[None, :]).astype(
        jnp.int32
    )
    earlier = jnp.cumsum(onehot, axis=0) - onehot
    position = jnp.sum(earlier * onehot, axis=1)
    slot_index = flat_ids * capacity + position
    placement = (slot_index[:, None] == jnp.arange(slot_count, dtype=jnp.int32)[None, :]).astype(
        jnp.bfloat16
    )
    repeated = jnp.repeat(dec_tokens, choices_per, axis=0)
    outgoing = jnp.einsum(
        "rs,rd->sd", placement, repeated, preferred_element_type=jnp.float32
    ).astype(jnp.bfloat16)
    arrived = lax.all_to_all(
        outgoing.reshape(expert_count, capacity, width),
        "exp",
        split_axis=0,
        concat_axis=0,
        tiled=True,
    )
    rows_in = arrived.reshape(slot_count, width)

    mixed = jnp.einsum(
        "dgf,sd->gfs", gate_up[0], rows_in, preferred_element_type=jnp.float32
    ).astype(jnp.bfloat16)
    units = mixed.shape[1] // shards
    mixed = mixed.reshape(2, shards, units, slot_count).transpose(1, 0, 2, 3)
    shares = lax.all_to_all(mixed, "dp", split_axis=0, concat_axis=0, tiled=True)
    shares = jnp.sum(shares.astype(jnp.float32), axis=0)
    hidden_part = (jax.nn.silu(shares[0]) * shares[1]).astype(jnp.bfloat16)
    hidden = lax.all_to_all(
        jnp.broadcast_to(hidden_part[None], (shards, units, slot_count)),
        "dp",
        split_axis=0,
        concat_axis=0,
        tiled=True,
    )

    theirs, ours = gradients(place, acts, parts)
    near = lax.ppermute(theirs, "dp", permutation(0, 0, 1))
    other = (1 - half) * RING
    crossing = lax.dynamic_slice_in_dim(ours, other, RING, 0) + lax.dynamic_slice_in_dim(
        near, other, RING, 0
    ).astype(jnp.float32)
    far = lax.ppermute(crossing.astype(jnp.bfloat16), "dp", permutation(1, 0, 0))
    tiles = adam_tiles(tokens, place, ours, near, far, parts)
    tiles = [
        tiles[0],
        lax.ppermute(tiles[1], "dp", permutation(0, 0, 1)),
        lax.ppermute(tiles[2], "dp", permutation(1, 0, 0)),
        lax.ppermute(tiles[3], "dp", permutation(1, 0, 1)),
    ]

    results = expert_results(place, hidden, tiles)
    returned = lax.all_to_all(
        results.reshape(expert_count, capacity, width),
        "exp",
        split_axis=0,
        concat_axis=0,
        tiled=True,
    )
    back_rows = returned.reshape(slot_count, width)
    chosen = jnp.einsum("rs,sd->rd", placement, back_rows, preferred_element_type=jnp.float32)
    weighted = chosen.reshape(token_count, choices_per, width) * route_gates[:, :, None]
    return jnp.sum(weighted, axis=1).astype(jnp.bfloat16)


def solution(mesh):
    in_specs = (
        P("exp", "dp", None),
        P("exp", "dp"),
        P("dp", None),
        P("exp", "dp", None),
        P("exp", "dp", None),
        P("exp", "dp", None),
        P("exp", "dp", None, None),
        P("exp", "dp"),
        P("exp", None),
        P("exp", None),
    )
    out_specs = P("exp", "dp")
    return jax.shard_map(body, mesh=mesh, in_specs=in_specs, out_specs=out_specs, check_vma=False)
```

```python
import functools

import jax
import jax.numpy as jnp
from jax import lax
from jax.experimental import pallas as pl
from jax.experimental.pallas import tpu as pltpu
from jax.sharding import PartitionSpec as P

beta_one = 0.9
beta_two = 0.95
learn_rate = 0.1
weight_decay = 0.1
epsilon = 1e-08
bias_first = 1.0 - 0.9**20
bias_second = 1.0 - 0.95**20

HALVES, RING, CORES = 2, 4, 2
SMEM = pl.BlockSpec(memory_space=pltpu.SMEM)
VMEM = pl.BlockSpec(memory_space=pltpu.VMEM)
PARAMS = pltpu.CompilerParams(vmem_limit_bytes=62 * 2**20)


def cost(flops, size):
    return pl.CostEstimate(flops=flops, bytes_accessed=size, transcendentals=0)


def whole(*shape):
    return pl.BlockSpec(shape, lambda *_: (0,) * len(shape))


def contract_first(left, right):
    return lax.dot_general(
        left, right, (((0,), (0,)), ((), ())), preferred_element_type=jnp.float32
    )


def permutation(half_step, ring_step, core_step):
    pairs = []
    for half in range(HALVES):
        for ring in range(RING):
            for core in range(CORES):
                source = (half * RING + ring) * CORES + core
                target = (half ^ half_step) * RING + (ring + ring_step) % RING
                pairs.append((source, target * CORES + (core ^ core_step)))
    return pairs


def pack_kernel(place_ref, rows_ref, grad_ref, master_ref, first_ref, second_ref, *outs):
    table, columns = grad_ref.shape
    tokens = rows_ref.shape[1]
    rows = master_ref.shape[1]
    width = columns // (HALVES * RING * CORES)
    onehot = (
        (lax.broadcasted_iota(jnp.int32, (table, tokens), 0) == rows_ref[...])
        .astype(jnp.float32)
        .astype(jnp.bfloat16)
    )
    ring = place_ref[1]
    for here in range(RING):

        @pl.when(ring == here)
        def _(here=here):
            for step in range(RING):
                out = outs[step]
                for core in range(CORES):
                    for half in range(HALVES):
                        owner = (half * RING + (here + step) % RING) * CORES + core
                        take = pl.ds(owner * width, width)
                        put = pl.ds((core * HALVES + half) * width, width)
                        out[0:tokens, put] = contract_first(onehot, grad_ref[:, take]).astype(
                            jnp.bfloat16
                        )
                        at = tokens
                        out[at : at + rows, put] = master_ref[0, :, take].astype(jnp.bfloat16)
                        out[at + rows : at + 2 * rows, put] = first_ref[0, :, take]
                        out[at + 2 * rows : at + 3 * rows, put] = second_ref[0, :, take]


def pack(place, train_rows, out_grad, master, moment1, moment2):
    tokens = train_rows.shape[1]
    rows = master.shape[1]
    shape = (tokens + 3 * rows, out_grad.shape[1] // RING)
    return pl.pallas_call(
        pack_kernel,
        out_shape=[jax.ShapeDtypeStruct(shape, jnp.bfloat16)] * RING,
        in_specs=[SMEM] + [VMEM] * 5,
        out_specs=[VMEM] * RING,
        compiler_params=PARAMS,
        cost_estimate=cost(2 * tokens * out_grad.size, 7_000_000),
    )(place, train_rows, out_grad, master, moment1, moment2)


def split(flag, values):
    width = values.shape[-1] // 2
    low, high = values[..., :width], values[..., width:]
    return jnp.where(flag == 0, low, high), jnp.where(flag == 0, high, low)


def gradient_kernel(place_ref, acts_ref, *refs):
    parts, (ours_ref, theirs_ref) = refs[:RING], refs[RING:]
    ring, core = place_ref[1], place_ref[2]
    acts = [acts_ref[(ring - step + RING) % RING] for step in range(RING)]
    total = None
    for step in range(0, RING, 2):
        left = jnp.concatenate([acts[step], acts[step + 1]], axis=0)
        right = jnp.concatenate([parts[step][...], parts[step + 1][...]], axis=0)
        product = contract_first(left, right)
        total = product if total is None else total + product
    ours, theirs = split(core, total)
    ours_ref[...] = ours
    theirs_ref[...] = theirs.astype(jnp.bfloat16).reshape(theirs_ref.shape)


def gradients(place, acts, parts):
    ring_tokens, units = acts.shape
    tokens = ring_tokens // RING
    width = parts[0].shape[1]
    block = units // 8
    return pl.pallas_call(
        gradient_kernel,
        grid=(8,),
        out_shape=[
            jax.ShapeDtypeStruct((units, width // 2), jnp.float32),
            jax.ShapeDtypeStruct((16, block // 2, width // 2), jnp.bfloat16),
        ],
        in_specs=[SMEM, pl.BlockSpec((RING, tokens, block), lambda i: (0, 0, i))]
        + [whole(tokens, width)] * RING,
        out_specs=[
            pl.BlockSpec((block, width // 2), lambda i: (i, 0)),
            pl.BlockSpec((2, block // 2, width // 2), lambda i: (i, 0, 0)),
        ],
        compiler_params=PARAMS,
        cost_estimate=cost(2 * units * width * ring_tokens, 5_000_000),
    )(place, acts.reshape(RING, tokens, units), *parts)


def cross_kernel(place_ref, ours_ref, near_ref, kept_ref, cross_ref):
    kept, cross = split(place_ref[0], ours_ref[...] + near_ref[...].astype(jnp.float32))
    kept_ref[...] = kept
    cross_ref[...] = cross.astype(jnp.bfloat16).reshape(cross_ref.shape)


def add_cores(place, ours, near):
    units, width = ours.shape
    block = units // 4
    return pl.pallas_call(
        cross_kernel,
        grid=(4,),
        out_shape=[
            jax.ShapeDtypeStruct((units, width // 2), jnp.float32),
            jax.ShapeDtypeStruct((16, block // 4, width // 2), jnp.bfloat16),
        ],
        in_specs=[SMEM] + [pl.BlockSpec((block, width), lambda i: (i, 0))] * 2,
        out_specs=[
            pl.BlockSpec((block, width // 2), lambda i: (i, 0)),
            pl.BlockSpec((4, block // 4, width // 2), lambda i: (i, 0, 0)),
        ],
        compiler_params=PARAMS,
        cost_estimate=cost(2 * ours.size, 4_000_000),
    )(place, ours, near)


def state_core_kernel(tokens, place_ref, *refs):
    parts, out_ref = refs[:RING], refs[RING]
    ring, core = place_ref[1], place_ref[2]
    for step in range(RING):
        out_ref[(ring - step + RING) % RING] = split(core, parts[step][tokens:, :])[1]


def states_for_core(place, parts, tokens):
    rows, width = parts[0].shape
    return pl.pallas_call(
        functools.partial(state_core_kernel, tokens),
        out_shape=jax.ShapeDtypeStruct((RING, rows - tokens, width // 2), jnp.bfloat16),
        in_specs=[SMEM] + [VMEM] * RING,
        out_specs=VMEM,
        compiler_params=PARAMS,
        cost_estimate=cost(0, 3_000_000),
    )(place, *parts)


def state_half_kernel(tokens, place_ref, near_ref, *refs):
    parts, (kept_ref, cross_ref) = refs[:RING], refs[RING:]
    half, ring, core = place_ref[0], place_ref[1], place_ref[2]
    for step in range(RING):
        mine = split(core, parts[step][tokens:, :])[0]
        source = (ring - step + RING) % RING
        kept, cross = split(half, mine)
        kept_ref[0, source] = kept
        cross_ref[0, source] = cross
        kept, cross = split(half, near_ref[step])
        kept_ref[1, step] = kept
        cross_ref[1, step] = cross


def states_for_half(place, near, parts, tokens):
    rows, width = parts[0].shape
    shape = (CORES, RING, rows - tokens, width // 4)
    return pl.pallas_call(
        functools.partial(state_half_kernel, tokens),
        out_shape=[jax.ShapeDtypeStruct(shape, jnp.bfloat16)] * 2,
        in_specs=[SMEM] + [VMEM] * (1 + RING),
        out_specs=[VMEM] * 2,
        compiler_params=PARAMS,
        cost_estimate=cost(0, 4_500_000),
    )(place, near, *parts)


def adam_kernel(place_ref, kept_ref, far_ref, near_states_ref, far_states_ref, tile_ref):
    half, core = place_ref[0], place_ref[2]
    rows = near_states_ref.shape[2] // 3
    for half_step in range(HALVES):
        states = (near_states_ref, far_states_ref)[half_step]
        for core_step in range(CORES):
            for ring in range(RING):
                source = (
                    jnp.bitwise_xor(half, half_step) * RING + ring
                ) * CORES + jnp.bitwise_xor(core, core_step)
                at = pl.ds(pl.multiple_of(source * rows, rows), rows)
                gradient = kept_ref[at, :] + far_ref[at, :].astype(jnp.float32)
                state = states[core_step, ring].astype(jnp.float32)
                master, first_old, second_old = (
                    state[k * rows : (k + 1) * rows] for k in range(3)
                )
                first = beta_one * first_old + (1.0 - beta_one) * gradient
                second = beta_two * second_old + (1.0 - beta_two) * gradient * gradient
                update = first / bias_first / (jnp.sqrt(second / bias_second) + epsilon)
                tile_ref[at, :] = (
                    master * (1.0 - learn_rate * weight_decay) - learn_rate * update
                ).astype(jnp.bfloat16)


def adam_tile(place, kept, far, near_states, far_states):
    return pl.pallas_call(
        adam_kernel,
        out_shape=jax.ShapeDtypeStruct(kept.shape, jnp.bfloat16),
        in_specs=[SMEM] + [VMEM] * 4,
        out_specs=VMEM,
        compiler_params=PARAMS,
        cost_estimate=cost(20 * kept.size, 4_000_000),
    )(place, kept, far, near_states, far_states)


def turn_kernel(mixed_ref, out_ref):
    gates, slots, units = mixed_ref.shape
    width = out_ref.shape[2]
    for gate in range(gates):
        for pair in range(units // (2 * width)):
            turned = mixed_ref[gate, :, pair * 2 * width : (pair + 1) * 2 * width].T
            turned = turned.astype(jnp.bfloat16)
            out_ref[2 * pair, gate] = turned[:width]
            out_ref[2 * pair + 1, gate] = turned[width:]


def turn(mixed, shards):
    gates, slots, units = mixed.shape
    return pl.pallas_call(
        turn_kernel,
        out_shape=jax.ShapeDtypeStruct((shards, gates, units // shards, slots), jnp.bfloat16),
        in_specs=[VMEM],
        out_specs=VMEM,
        compiler_params=PARAMS,
        cost_estimate=cost(0, 1_500_000),
    )(mixed)


def hidden_kernel(shares_ref, out_ref):
    sums = jnp.sum(shares_ref[...].astype(jnp.float32), axis=0)
    hidden = (jax.nn.silu(sums[0]) * sums[1]).astype(jnp.bfloat16)
    for shard in range(out_ref.shape[0]):
        out_ref[shard] = hidden


def hidden_units(shares):
    shards, _, units, slots = shares.shape
    return pl.pallas_call(
        hidden_kernel,
        out_shape=jax.ShapeDtypeStruct((shards, units, slots), jnp.bfloat16),
        in_specs=[VMEM],
        out_specs=VMEM,
        compiler_params=PARAMS,
        cost_estimate=cost(shares.size, 800_000),
    )(shares)


def results_kernel(hidden_ref, tile_ref, out_ref):
    out_ref[...] = contract_first(hidden_ref[...], tile_ref[...]).astype(jnp.bfloat16)


def expert_results(hidden, tile):
    return pl.pallas_call(
        results_kernel,
        out_shape=jax.ShapeDtypeStruct((hidden.shape[1], tile.shape[1]), jnp.bfloat16),
        in_specs=[VMEM] * 2,
        out_specs=VMEM,
        compiler_params=PARAMS,
        cost_estimate=cost(2 * hidden.size * tile.shape[1], 800_000),
    )(hidden, tile)


def body(
    hidden_acts,
    train_rows,
    out_grad,
    master,
    moment1,
    moment2,
    gate_up,
    dec_tokens,
    route_ids,
    route_gates,
):
    index = lax.axis_index("dp")
    shards = lax.axis_size("dp")
    half, ring, core = index >> 3, (index >> 1) & (RING - 1), index & (CORES - 1)
    place = jnp.stack([half, ring, core]).astype(jnp.int32)
    token_count, width = dec_tokens.shape
    tokens = train_rows.shape[1]

    rings = [
        [(h * RING + r) * CORES + c for r in range(RING)]
        for h in range(HALVES)
        for c in range(CORES)
    ]
    acts = lax.all_gather(hidden_acts[0], "dp", axis=0, tiled=True, axis_index_groups=rings)
    sends = pack(place, train_rows, out_grad, master, moment1, moment2)
    parts = [sends[0]] + [
        lax.ppermute(sends[step], "dp", permutation(0, step, 0)) for step in range(1, RING)
    ]

    choices_per = route_ids.shape[1]
    expert_count = lax.axis_size("exp")
    capacity = min(token_count, max(2, 2 * choices_per * token_count // expert_count))
    slot_count = expert_count * capacity
    flat_ids = route_ids.reshape(-1)
    onehot = (flat_ids[:, None] == jnp.arange(expert_count, dtype=jnp.int32)[None, :]).astype(
        jnp.int32
    )
    earlier = jnp.cumsum(onehot, axis=0) - onehot
    position = jnp.sum(earlier * onehot, axis=1)
    slot_index = flat_ids * capacity + position
    placement = (slot_index[:, None] == jnp.arange(slot_count, dtype=jnp.int32)[None, :]).astype(
        jnp.bfloat16
    )
    repeated = jnp.repeat(dec_tokens, choices_per, axis=0)
    outgoing = jnp.einsum(
        "rs,rd->sd", placement, repeated, preferred_element_type=jnp.float32
    ).astype(jnp.bfloat16)
    arrived = lax.all_to_all(
        outgoing.reshape(expert_count, capacity, width),
        "exp",
        split_axis=0,
        concat_axis=0,
        tiled=True,
    )
    rows_in = arrived.reshape(slot_count, width)

    mixed = jnp.einsum(
        "dgf,sd->gsf", gate_up[0], rows_in, preferred_element_type=jnp.float32
    )
    shares = lax.all_to_all(
        turn(mixed, shards), "dp", split_axis=0, concat_axis=0, tiled=True
    )
    hidden = lax.all_to_all(
        hidden_units(shares), "dp", split_axis=0, concat_axis=0, tiled=True
    ).reshape(-1, slot_count)

    across_cores, across_halves = permutation(0, 0, 1), permutation(1, 0, 0)
    ours, theirs = gradients(place, acts, parts)
    near = lax.ppermute(theirs, "dp", across_cores).reshape(ours.shape)
    near_states = lax.ppermute(states_for_core(place, parts, tokens), "dp", across_cores)
    kept_states, cross_states = states_for_half(place, near_states, parts, tokens)
    far_states = lax.ppermute(cross_states, "dp", across_halves)
    kept, cross = add_cores(place, ours, near)
    far = lax.ppermute(cross, "dp", across_halves).reshape(kept.shape)
    tile = adam_tile(place, kept, far, kept_states, far_states)

    results = expert_results(hidden, tile)
    returned = lax.all_to_all(
        results.reshape(expert_count, capacity, width),
        "exp",
        split_axis=0,
        concat_axis=0,
        tiled=True,
    )
    back_rows = returned.reshape(slot_count, width)
    chosen = jnp.einsum("rs,sd->rd", placement, back_rows, preferred_element_type=jnp.float32)
    weighted = chosen.reshape(token_count, choices_per, width) * route_gates[:, :, None]
    return jnp.sum(weighted, axis=1).astype(jnp.bfloat16)


def solution(mesh):
    in_specs = (
        P("exp", "dp", None),
        P("exp", "dp"),
        P("dp", None),
        P("exp", "dp", None),
        P("exp", "dp", None),
        P("exp", "dp", None),
        P("exp", "dp", None, None),
        P("exp", "dp"),
        P("exp", None),
        P("exp", None),
    )
    out_specs = P("exp", "dp")
    return jax.shard_map(body, mesh=mesh, in_specs=in_specs, out_specs=out_specs, check_vma=False)
```

```python
import functools

import jax
import jax.numpy as jnp
from jax import lax
from jax.experimental import pallas as pl
from jax.experimental.pallas import tpu as pltpu
from jax.sharding import PartitionSpec as P

beta_one = 0.9
beta_two = 0.95
learn_rate = 0.1
weight_decay = 0.1
epsilon = 1e-08
bias_first = 1.0 - 0.9**20
bias_second = 1.0 - 0.95**20

HALVES, RING, CORES = 2, 4, 2
PIECES = 4
SMEM = pl.BlockSpec(memory_space=pltpu.SMEM)
VMEM = pl.BlockSpec(memory_space=pltpu.VMEM)
PARAMS = pltpu.CompilerParams(vmem_limit_bytes=62 * 2**20)
SMALL = pltpu.CompilerParams(vmem_limit_bytes=24 * 2**20)


def cost(flops, size):
    return pl.CostEstimate(flops=flops, bytes_accessed=size, transcendentals=0)


def whole(*shape):
    return pl.BlockSpec(shape, lambda *_: (0,) * len(shape))


def contract_first(left, right):
    return lax.dot_general(
        left, right, (((0,), (0,)), ((), ())), preferred_element_type=jnp.float32
    )


def permutation(half_step, ring_step, core_step):
    pairs = []
    for half in range(HALVES):
        for ring in range(RING):
            for core in range(CORES):
                source = (half * RING + ring) * CORES + core
                target = (half ^ half_step) * RING + (ring + ring_step) % RING
                pairs.append((source, target * CORES + (core ^ core_step)))
    return pairs


def pack_kernel(place_ref, rows_ref, grad_ref, master_ref, first_ref, second_ref, *outs):
    table, columns = grad_ref.shape
    tokens = rows_ref.shape[1]
    rows = master_ref.shape[1]
    owners = HALVES * RING * CORES // PIECES
    width = columns // owners
    onehot = (
        (lax.broadcasted_iota(jnp.int32, (table, tokens), 0) == rows_ref[...])
        .astype(jnp.float32)
        .astype(jnp.bfloat16)
    )
    ring = place_ref[1]
    for here in range(RING):
        for piece in range(PIECES):

            @pl.when((ring == here) & (pl.program_id(0) == piece))
            def _(here=here, piece=piece):
                for local in range(owners):
                    owner = piece * owners + local
                    half, place = owner // (RING * CORES), owner // CORES % RING
                    out = outs[(place - here) % RING]
                    take = pl.ds(local * width, width)
                    put = pl.ds((owner % CORES * HALVES + half) * width, width)
                    out[0:tokens, put] = contract_first(onehot, grad_ref[:, take]).astype(
                        jnp.bfloat16
                    )
                    at = tokens
                    out[at : at + rows, put] = master_ref[0, :, take].astype(jnp.bfloat16)
                    out[at + rows : at + 2 * rows, put] = first_ref[0, :, take]
                    out[at + 2 * rows : at + 3 * rows, put] = second_ref[0, :, take]


def pack(place, train_rows, out_grad, master, moment1, moment2):
    tokens = train_rows.shape[1]
    rows = master.shape[1]
    table, columns = out_grad.shape
    shape = (tokens + 3 * rows, columns // RING)
    state = pl.BlockSpec((1, rows, columns // PIECES), lambda i: (0, 0, i))
    return pl.pallas_call(
        pack_kernel,
        grid=(PIECES,),
        out_shape=[jax.ShapeDtypeStruct(shape, jnp.bfloat16)] * RING,
        in_specs=[
            SMEM,
            whole(1, tokens),
            pl.BlockSpec((table, columns // PIECES), lambda i: (0, i)),
            state,
            state,
            state,
        ],
        out_specs=[whole(*shape)] * RING,
        compiler_params=PARAMS,
        cost_estimate=cost(2 * tokens * out_grad.size, 7_000_000),
    )(place, train_rows, out_grad, master, moment1, moment2)


def split(flag, values):
    width = values.shape[-1] // 2
    low, high = values[..., :width], values[..., width:]
    return jnp.where(flag == 0, low, high), jnp.where(flag == 0, high, low)


def core_kernel(place_ref, *refs):
    parts, (mine_ref, theirs_ref) = refs[:RING], refs[RING:]
    ring, core = place_ref[1], place_ref[2]
    for step in range(RING):
        mine, theirs = split(core, parts[step][...])
        source = (ring - step + RING) % RING
        mine_ref[source] = mine
        theirs_ref[source] = theirs


def split_cores(place, parts):
    rows, width = parts[0].shape
    block = 64
    return pl.pallas_call(
        core_kernel,
        grid=(rows // block,),
        out_shape=[jax.ShapeDtypeStruct((RING, rows, width // 2), jnp.bfloat16)] * 2,
        in_specs=[SMEM] + [pl.BlockSpec((block, width), lambda i: (i, 0))] * RING,
        out_specs=[pl.BlockSpec((RING, block, width // 2), lambda i: (0, i, 0))] * 2,
        compiler_params=PARAMS,
        cost_estimate=cost(0, 5_000_000),
    )(place, *parts)


def gradient_kernel(place_ref, acts_ref, mine_ref, near_ref, out_ref):
    core = place_ref[2]
    total = None
    for ring in range(RING):
        left = jnp.concatenate(
            [acts_ref[ring * CORES + core], acts_ref[ring * CORES + 1 - core]], axis=0
        )
        right = jnp.concatenate([mine_ref[ring], near_ref[ring]], axis=0)
        product = contract_first(left, right)
        total = product if total is None else total + product
    out_ref[...] = total.astype(out_ref.dtype).reshape(out_ref.shape)


def gradient_rows(place, acts, mine, near, tokens, other_half, dtype):
    group_tokens, units = acts.shape
    sources = RING * CORES
    blocks = 2
    block = units // HALVES // blocks
    width = mine.shape[2]
    rows = units // HALVES // sources
    operand = pl.BlockSpec((RING, tokens, width), lambda i, place: (0, 0, 0))
    return pl.pallas_call(
        gradient_kernel,
        out_shape=jax.ShapeDtypeStruct((sources, rows, width), dtype),
        grid_spec=pltpu.PrefetchScalarGridSpec(
            num_scalar_prefetch=1,
            grid=(blocks,),
            in_specs=[
                pl.BlockSpec(
                    (sources, tokens, block),
                    lambda i, place: (
                        0,
                        0,
                        jnp.bitwise_xor(place[0], other_half) * blocks + i,
                    ),
                ),
                operand,
                operand,
            ],
            out_specs=pl.BlockSpec(
                (sources // blocks, rows, width), lambda i, place: (i, 0, 0)
            ),
        ),
        compiler_params=PARAMS,
        cost_estimate=cost(2 * block * blocks * width * group_tokens, 4_000_000),
    )(place, acts.reshape(sources, tokens, units), mine, near)


def adam_kernel(tokens, place_ref, kept_ref, far_ref, mine_ref, near_ref, tile_ref):
    rows = kept_ref.shape[1]
    for step, states in enumerate((mine_ref, near_ref)):
        core = jnp.bitwise_xor(place_ref[2], step)
        gradient = kept_ref[core] + far_ref[core].astype(jnp.float32)
        master, first_old, second_old = (
            states[0, tokens + k * rows : tokens + (k + 1) * rows, :].astype(jnp.float32)
            for k in range(3)
        )
        first = beta_one * first_old + (1.0 - beta_one) * gradient
        second = beta_two * second_old + (1.0 - beta_two) * gradient * gradient
        update = first / bias_first / (jnp.sqrt(second / bias_second) + epsilon)
        tile_ref[core] = (
            master * (1.0 - learn_rate * weight_decay) - learn_rate * update
        ).astype(jnp.bfloat16)


def adam_tile(tokens, place, kept, far, mine, near):
    sources, rows, width = kept.shape
    pair = pl.BlockSpec((CORES, rows, width), lambda i: (i, 0, 0))
    states = pl.BlockSpec((1, mine.shape[1], width), lambda i: (i, 0, 0))
    return pl.pallas_call(
        functools.partial(adam_kernel, tokens),
        grid=(RING,),
        out_shape=jax.ShapeDtypeStruct(kept.shape, jnp.bfloat16),
        in_specs=[SMEM, pair, pair, states, states],
        out_specs=pair,
        compiler_params=PARAMS,
        cost_estimate=cost(20 * kept.size, 5_000_000),
    )(place, kept, far, mine, near)


def turn_kernel(mixed_ref, out_ref):
    gates, slots, units = mixed_ref.shape
    width = out_ref.shape[2]
    for gate in range(gates):
        for pair in range(units // (2 * width)):
            turned = mixed_ref[gate, :, pair * 2 * width : (pair + 1) * 2 * width].T
            turned = turned.astype(jnp.bfloat16)
            out_ref[2 * pair, gate] = turned[:width]
            out_ref[2 * pair + 1, gate] = turned[width:]


def turn(mixed, shards):
    gates, slots, units = mixed.shape
    return pl.pallas_call(
        turn_kernel,
        out_shape=jax.ShapeDtypeStruct((shards, gates, units // shards, slots), jnp.bfloat16),
        in_specs=[VMEM],
        out_specs=VMEM,
        compiler_params=SMALL,
        cost_estimate=cost(0, 1_500_000),
    )(mixed)


def hidden_kernel(shares_ref, out_ref):
    sums = jnp.sum(shares_ref[...].astype(jnp.float32), axis=0)
    hidden = (jax.nn.silu(sums[0]) * sums[1]).astype(jnp.bfloat16)
    for shard in range(out_ref.shape[0]):
        out_ref[shard] = hidden


def hidden_units(shares, copies):
    _, _, units, slots = shares.shape
    return pl.pallas_call(
        hidden_kernel,
        out_shape=jax.ShapeDtypeStruct((copies, units, slots), jnp.bfloat16),
        in_specs=[VMEM],
        out_specs=VMEM,
        compiler_params=SMALL,
        cost_estimate=cost(shares.size, 800_000),
    )(shares)


def results_kernel(place_ref, hidden_ref, tile_ref, kept_ref, cross_ref):
    total = contract_first(hidden_ref[...], tile_ref[...])
    kept, cross = split(place_ref[0], total)
    kept_ref[...] = kept.reshape(kept_ref.shape)
    cross_ref[...] = cross.astype(jnp.bfloat16).reshape(cross_ref.shape)


def expert_results(place, hidden, tile):
    shape = (2, hidden.shape[1] // 2, tile.shape[1] // 2)
    return pl.pallas_call(
        results_kernel,
        out_shape=[
            jax.ShapeDtypeStruct(shape, jnp.float32),
            jax.ShapeDtypeStruct(shape, jnp.bfloat16),
        ],
        in_specs=[SMEM, VMEM, VMEM],
        out_specs=[VMEM] * 2,
        compiler_params=SMALL,
        cost_estimate=cost(2 * hidden.size * tile.shape[1], 900_000),
    )(place, hidden, tile)


def body(
    hidden_acts,
    train_rows,
    out_grad,
    master,
    moment1,
    moment2,
    gate_up,
    dec_tokens,
    route_ids,
    route_gates,
):
    index = lax.axis_index("dp")
    shards = lax.axis_size("dp")
    half, ring, core = index >> 3, (index >> 1) & (RING - 1), index & (CORES - 1)
    place = jnp.stack([half, ring, core]).astype(jnp.int32)
    token_count, width = dec_tokens.shape
    tokens = train_rows.shape[1]

    sides = [[h * RING * CORES + k for k in range(RING * CORES)] for h in range(HALVES)]
    acts = lax.all_gather(hidden_acts[0], "dp", axis=0, tiled=True, axis_index_groups=sides)
    sends = pack(place, train_rows, out_grad, master, moment1, moment2)
    parts = [sends[0]] + [
        lax.ppermute(sends[step], "dp", permutation(0, step, 0)) for step in range(1, RING)
    ]

    choices_per = route_ids.shape[1]
    expert_count = lax.axis_size("exp")
    capacity = min(token_count, max(2, 2 * choices_per * token_count // expert_count))
    slot_count = expert_count * capacity
    flat_ids = route_ids.reshape(-1)
    onehot = (flat_ids[:, None] == jnp.arange(expert_count, dtype=jnp.int32)[None, :]).astype(
        jnp.int32
    )
    earlier = jnp.cumsum(onehot, axis=0) - onehot
    position = jnp.sum(earlier * onehot, axis=1)
    slot_index = flat_ids * capacity + position
    placement = (slot_index[:, None] == jnp.arange(slot_count, dtype=jnp.int32)[None, :]).astype(
        jnp.bfloat16
    )
    repeated = jnp.repeat(dec_tokens, choices_per, axis=0)
    outgoing = jnp.einsum(
        "rs,rd->sd", placement, repeated, preferred_element_type=jnp.float32
    ).astype(jnp.bfloat16)
    arrived = lax.all_to_all(
        outgoing.reshape(expert_count, capacity, width),
        "exp",
        split_axis=0,
        concat_axis=0,
        tiled=True,
    )
    rows_in = arrived.reshape(slot_count, width)

    mixed = jnp.einsum(
        "dgf,sd->gsf", gate_up[0], rows_in, preferred_element_type=jnp.float32
    )
    shares = lax.all_to_all(
        turn(mixed, shards), "dp", split_axis=0, concat_axis=0, tiled=True
    )
    hidden = lax.all_to_all(
        hidden_units(shares, RING * CORES),
        "dp",
        split_axis=0,
        concat_axis=0,
        tiled=True,
        axis_index_groups=sides,
    ).reshape(-1, slot_count)

    across_cores, across_halves = permutation(0, 0, 1), permutation(1, 0, 0)
    mine, theirs = split_cores(place, parts)
    near = lax.ppermute(theirs, "dp", across_cores)
    cross = gradient_rows(place, acts, mine, near, tokens, 1, jnp.bfloat16)
    far = lax.ppermute(cross, "dp", across_halves)
    kept = gradient_rows(place, acts, mine, near, tokens, 0, jnp.float32)
    tile = adam_tile(tokens, place, kept, far, mine, near)

    kept_results, cross_results = expert_results(place, hidden, tile.reshape(-1, 2 * width))
    far_results = lax.ppermute(cross_results, "dp", across_halves)
    results = (kept_results + far_results.astype(jnp.float32)).astype(jnp.bfloat16)
    returned = lax.all_to_all(
        results.reshape(expert_count, capacity, width),
        "exp",
        split_axis=0,
        concat_axis=0,
        tiled=True,
    )
    back_rows = returned.reshape(slot_count, width)
    chosen = jnp.einsum("rs,sd->rd", placement, back_rows, preferred_element_type=jnp.float32)
    weighted = chosen.reshape(token_count, choices_per, width) * route_gates[:, :, None]
    return jnp.sum(weighted, axis=1).astype(jnp.bfloat16)


def solution(mesh):
    in_specs = (
        P("exp", "dp", None),
        P("exp", "dp"),
        P("dp", None),
        P("exp", "dp", None),
        P("exp", "dp", None),
        P("exp", "dp", None),
        P("exp", "dp", None, None),
        P("exp", "dp"),
        P("exp", None),
        P("exp", None),
    )
    out_specs = P("exp", "dp")
    return jax.shard_map(body, mesh=mesh, in_specs=in_specs, out_specs=out_specs, check_vma=False)
```

```python
import functools

import jax
import jax.numpy as jnp
from jax import lax
from jax.experimental import pallas as pl
from jax.experimental.pallas import tpu as pltpu
from jax.sharding import PartitionSpec as P

beta_one = 0.9
beta_two = 0.95
learn_rate = 0.1
weight_decay = 0.1
epsilon = 1e-08
bias_first = 1.0 - 0.9**20
bias_second = 1.0 - 0.95**20

HALVES, RING, CORES = 2, 4, 2
PIECES = 4
SMEM = pl.BlockSpec(memory_space=pltpu.SMEM)
VMEM = pl.BlockSpec(memory_space=pltpu.VMEM)
PARAMS = pltpu.CompilerParams(vmem_limit_bytes=62 * 2**20)
SMALL = pltpu.CompilerParams(vmem_limit_bytes=24 * 2**20)


def cost(flops, size):
    return pl.CostEstimate(flops=flops, bytes_accessed=size, transcendentals=0)


def whole(*shape):
    return pl.BlockSpec(shape, lambda *_: (0,) * len(shape))


def contract_first(left, right):
    return lax.dot_general(
        left, right, (((0,), (0,)), ((), ())), preferred_element_type=jnp.float32
    )


def permutation(half_step, ring_step, core_step):
    pairs = []
    for half in range(HALVES):
        for ring in range(RING):
            for core in range(CORES):
                source = (half * RING + ring) * CORES + core
                target = (half ^ half_step) * RING + (ring + ring_step) % RING
                pairs.append((source, target * CORES + (core ^ core_step)))
    return pairs


def pack_kernel(place_ref, rows_ref, grad_ref, master_ref, first_ref, second_ref, *outs):
    table, columns = grad_ref.shape
    tokens = rows_ref.shape[1]
    rows = master_ref.shape[1]
    owners = HALVES * RING * CORES // PIECES
    width = columns // owners
    onehot = (
        (lax.broadcasted_iota(jnp.int32, (table, tokens), 0) == rows_ref[...])
        .astype(jnp.float32)
        .astype(jnp.bfloat16)
    )
    ring = place_ref[1]
    for here in range(RING):
        for piece in range(PIECES):

            @pl.when((ring == here) & (pl.program_id(0) == piece))
            def _(here=here, piece=piece):
                for local in range(owners):
                    owner = piece * owners + local
                    half, place = owner // (RING * CORES), owner // CORES % RING
                    out = outs[(place - here) % RING]
                    take = pl.ds(local * width, width)
                    put = pl.ds((owner % CORES * HALVES + half) * width, width)
                    out[0:tokens, put] = contract_first(onehot, grad_ref[:, take]).astype(
                        jnp.bfloat16
                    )
                    at = tokens
                    out[at : at + rows, put] = master_ref[0, :, take].astype(jnp.bfloat16)
                    out[at + rows : at + 2 * rows, put] = first_ref[0, :, take]
                    out[at + 2 * rows : at + 3 * rows, put] = second_ref[0, :, take]


def pack(place, train_rows, out_grad, master, moment1, moment2):
    tokens = train_rows.shape[1]
    rows = master.shape[1]
    table, columns = out_grad.shape
    shape = (tokens + 3 * rows, columns // RING)
    state = pl.BlockSpec((1, rows, columns // PIECES), lambda i: (0, 0, i))
    return pl.pallas_call(
        pack_kernel,
        grid=(PIECES,),
        out_shape=[jax.ShapeDtypeStruct(shape, jnp.bfloat16)] * RING,
        in_specs=[
            SMEM,
            whole(1, tokens),
            pl.BlockSpec((table, columns // PIECES), lambda i: (0, i)),
            state,
            state,
            state,
        ],
        out_specs=[whole(*shape)] * RING,
        compiler_params=PARAMS,
        cost_estimate=cost(2 * tokens * out_grad.size, 7_000_000),
    )(place, train_rows, out_grad, master, moment1, moment2)


def split(flag, values):
    width = values.shape[-1] // 2
    low, high = values[..., :width], values[..., width:]
    return jnp.where(flag == 0, low, high), jnp.where(flag == 0, high, low)


def core_kernel(place_ref, *refs):
    parts, (mine_ref, theirs_ref) = refs[:RING], refs[RING:]
    ring, core = place_ref[1], place_ref[2]
    for step in range(RING):
        mine, theirs = split(core, parts[step][...])
        source = (ring - step + RING) % RING
        mine_ref[source] = mine
        theirs_ref[source] = theirs


def split_cores(place, parts):
    rows, width = parts[0].shape
    block = 64
    return pl.pallas_call(
        core_kernel,
        grid=(rows // block,),
        out_shape=[jax.ShapeDtypeStruct((RING, rows, width // 2), jnp.bfloat16)] * 2,
        in_specs=[SMEM] + [pl.BlockSpec((block, width), lambda i: (i, 0))] * RING,
        out_specs=[pl.BlockSpec((RING, block, width // 2), lambda i: (0, i, 0))] * 2,
        compiler_params=PARAMS,
        cost_estimate=cost(0, 5_000_000),
    )(place, *parts)


def gradient_kernel(place_ref, acts_ref, mine_ref, near_ref, out_ref):
    core = place_ref[2]
    total = None
    for ring in range(RING):
        left = jnp.concatenate(
            [acts_ref[ring * CORES + core], acts_ref[ring * CORES + 1 - core]], axis=0
        )
        right = jnp.concatenate([mine_ref[ring], near_ref[ring]], axis=0)
        product = contract_first(left, right)
        total = product if total is None else total + product
    out_ref[...] = total.astype(out_ref.dtype).reshape(out_ref.shape)


def gradient_rows(place, acts, mine, near, tokens, other_half, dtype):
    group_tokens, units = acts.shape
    sources = RING * CORES
    blocks = 2
    block = units // HALVES // blocks
    width = mine.shape[2]
    rows = units // HALVES // sources
    operand = pl.BlockSpec((RING, tokens, width), lambda i, place: (0, 0, 0))
    return pl.pallas_call(
        gradient_kernel,
        out_shape=jax.ShapeDtypeStruct((sources, rows, width), dtype),
        grid_spec=pltpu.PrefetchScalarGridSpec(
            num_scalar_prefetch=1,
            grid=(blocks,),
            in_specs=[
                pl.BlockSpec(
                    (sources, tokens, block),
                    lambda i, place: (
                        0,
                        0,
                        jnp.bitwise_xor(place[0], other_half) * blocks + i,
                    ),
                ),
                operand,
                operand,
            ],
            out_specs=pl.BlockSpec(
                (sources // blocks, rows, width), lambda i, place: (i, 0, 0)
            ),
        ),
        compiler_params=PARAMS,
        cost_estimate=cost(2 * block * blocks * width * group_tokens, 4_000_000),
    )(place, acts.reshape(sources, tokens, units), mine, near)


def adam_kernel(tokens, place_ref, kept_ref, far_ref, mine_ref, near_ref, tile_ref):
    rows = kept_ref.shape[1]
    for step, states in enumerate((mine_ref, near_ref)):
        core = jnp.bitwise_xor(place_ref[2], step)
        gradient = kept_ref[core] + far_ref[core].astype(jnp.float32)
        master, first_old, second_old = (
            states[0, tokens + k * rows : tokens + (k + 1) * rows, :].astype(jnp.float32)
            for k in range(3)
        )
        first = beta_one * first_old + (1.0 - beta_one) * gradient
        second = beta_two * second_old + (1.0 - beta_two) * gradient * gradient
        update = first / bias_first / (jnp.sqrt(second / bias_second) + epsilon)
        tile_ref[core] = (
            master * (1.0 - learn_rate * weight_decay) - learn_rate * update
        ).astype(jnp.bfloat16)


def adam_tile(tokens, place, kept, far, mine, near):
    sources, rows, width = kept.shape
    pair = pl.BlockSpec((CORES, rows, width), lambda i: (i, 0, 0))
    states = pl.BlockSpec((1, mine.shape[1], width), lambda i: (i, 0, 0))
    return pl.pallas_call(
        functools.partial(adam_kernel, tokens),
        grid=(RING,),
        out_shape=jax.ShapeDtypeStruct(kept.shape, jnp.bfloat16),
        in_specs=[SMEM, pair, pair, states, states],
        out_specs=pair,
        compiler_params=PARAMS,
        cost_estimate=cost(20 * kept.size, 5_000_000),
    )(place, kept, far, mine, near)


def turn_kernel(mixed_ref, out_ref):
    gates, slots, units = mixed_ref.shape
    width = out_ref.shape[2]
    for gate in range(gates):
        for pair in range(units // (2 * width)):
            turned = mixed_ref[gate, :, pair * 2 * width : (pair + 1) * 2 * width].T
            turned = turned.astype(jnp.bfloat16)
            out_ref[2 * pair, gate] = turned[:width]
            out_ref[2 * pair + 1, gate] = turned[width:]


def turn(mixed, shards):
    gates, slots, units = mixed.shape
    return pl.pallas_call(
        turn_kernel,
        out_shape=jax.ShapeDtypeStruct((shards, gates, units // shards, slots), jnp.bfloat16),
        in_specs=[VMEM],
        out_specs=VMEM,
        compiler_params=SMALL,
        cost_estimate=cost(0, 1_500_000),
    )(mixed)


def hidden_kernel(shares_ref, out_ref):
    sums = jnp.sum(shares_ref[...].astype(jnp.float32), axis=0)
    hidden = (jax.nn.silu(sums[0]) * sums[1]).astype(jnp.bfloat16)
    for shard in range(out_ref.shape[0]):
        out_ref[shard] = hidden


def hidden_units(shares, copies):
    _, _, units, slots = shares.shape
    return pl.pallas_call(
        hidden_kernel,
        out_shape=jax.ShapeDtypeStruct((copies, units, slots), jnp.bfloat16),
        in_specs=[VMEM],
        out_specs=VMEM,
        compiler_params=SMALL,
        cost_estimate=cost(shares.size, 800_000),
    )(shares)


def results_kernel(place_ref, hidden_ref, tile_ref, kept_ref, cross_ref):
    total = contract_first(hidden_ref[...], tile_ref[...])
    kept, cross = split(place_ref[0], total)
    kept_ref[...] = kept.reshape(kept_ref.shape)
    cross_ref[...] = cross.astype(jnp.bfloat16).reshape(cross_ref.shape)


def expert_results(place, hidden, tile):
    shape = (2, hidden.shape[1] // 2, tile.shape[1] // 2)
    return pl.pallas_call(
        results_kernel,
        out_shape=[
            jax.ShapeDtypeStruct(shape, jnp.float32),
            jax.ShapeDtypeStruct(shape, jnp.bfloat16),
        ],
        in_specs=[SMEM, VMEM, VMEM],
        out_specs=[VMEM] * 2,
        compiler_params=SMALL,
        cost_estimate=cost(2 * hidden.size * tile.shape[1], 900_000),
    )(place, hidden, tile)


def body(
    hidden_acts,
    train_rows,
    out_grad,
    master,
    moment1,
    moment2,
    gate_up,
    dec_tokens,
    route_ids,
    route_gates,
):
    index = lax.axis_index("dp")
    shards = lax.axis_size("dp")
    half, ring, core = index >> 3, (index >> 1) & (RING - 1), index & (CORES - 1)
    place = jnp.stack([half, ring, core]).astype(jnp.int32)
    token_count, width = dec_tokens.shape
    tokens = train_rows.shape[1]

    sides = [[h * RING * CORES + k for k in range(RING * CORES)] for h in range(HALVES)]
    acts = lax.all_gather(hidden_acts[0], "dp", axis=0, tiled=True, axis_index_groups=sides)
    sends = pack(place, train_rows, out_grad, master, moment1, moment2)
    parts = [sends[0]] + [
        lax.ppermute(sends[step], "dp", permutation(0, step, 0)) for step in range(1, RING)
    ]

    choices_per = route_ids.shape[1]
    expert_count = lax.axis_size("exp")
    capacity = min(token_count, max(2, 2 * choices_per * token_count // expert_count))
    slot_count = expert_count * capacity
    flat_ids = route_ids.reshape(-1)
    onehot = (flat_ids[:, None] == jnp.arange(expert_count, dtype=jnp.int32)[None, :]).astype(
        jnp.int32
    )
    earlier = jnp.cumsum(onehot, axis=0) - onehot
    position = jnp.sum(earlier * onehot, axis=1)
    slot_index = flat_ids * capacity + position
    placement = (slot_index[:, None] == jnp.arange(slot_count, dtype=jnp.int32)[None, :]).astype(
        jnp.bfloat16
    )
    repeated = jnp.repeat(dec_tokens, choices_per, axis=0)
    outgoing = jnp.einsum(
        "rs,rd->sd", placement, repeated, preferred_element_type=jnp.float32
    ).astype(jnp.bfloat16)
    arrived = lax.all_to_all(
        outgoing.reshape(expert_count, capacity, width),
        "exp",
        split_axis=0,
        concat_axis=0,
        tiled=True,
    )
    arrived, held = lax.optimization_barrier((arrived, parts))
    rows_in = arrived.reshape(slot_count, width)

    mixed = jnp.einsum(
        "dgf,sd->gsf", gate_up[0], rows_in, preferred_element_type=jnp.float32
    )
    shares = lax.all_to_all(
        turn(mixed, shards), "dp", split_axis=0, concat_axis=0, tiled=True
    )
    hidden = lax.all_to_all(
        hidden_units(shares, RING * CORES),
        "dp",
        split_axis=0,
        concat_axis=0,
        tiled=True,
        axis_index_groups=sides,
    ).reshape(-1, slot_count)

    across_cores, across_halves = permutation(0, 0, 1), permutation(1, 0, 0)
    mine, theirs = split_cores(place, held)
    near = lax.ppermute(theirs, "dp", across_cores)
    cross = gradient_rows(place, acts, mine, near, tokens, 1, jnp.bfloat16)
    far = lax.ppermute(cross, "dp", across_halves)
    kept = gradient_rows(place, acts, mine, near, tokens, 0, jnp.float32)
    tile = adam_tile(tokens, place, kept, far, mine, near)

    kept_results, cross_results = expert_results(place, hidden, tile.reshape(-1, 2 * width))
    far_results = lax.ppermute(cross_results, "dp", across_halves)
    results = (kept_results + far_results.astype(jnp.float32)).astype(jnp.bfloat16)
    returned = lax.all_to_all(
        results.reshape(expert_count, capacity, width),
        "exp",
        split_axis=0,
        concat_axis=0,
        tiled=True,
    )
    back_rows = returned.reshape(slot_count, width)
    chosen = jnp.einsum("rs,sd->rd", placement, back_rows, preferred_element_type=jnp.float32)
    weighted = chosen.reshape(token_count, choices_per, width) * route_gates[:, :, None]
    return jnp.sum(weighted, axis=1).astype(jnp.bfloat16)


def solution(mesh):
    in_specs = (
        P("exp", "dp", None),
        P("exp", "dp"),
        P("dp", None),
        P("exp", "dp", None),
        P("exp", "dp", None),
        P("exp", "dp", None),
        P("exp", "dp", None, None),
        P("exp", "dp"),
        P("exp", None),
        P("exp", None),
    )
    out_specs = P("exp", "dp")
    return jax.shard_map(body, mesh=mesh, in_specs=in_specs, out_specs=out_specs, check_vma=False)
```

```python
import functools

import jax
import jax.numpy as jnp
from jax import lax
from jax.experimental import pallas as pl
from jax.experimental.pallas import tpu as pltpu
from jax.sharding import PartitionSpec as P

beta_one = 0.9
beta_two = 0.95
learn_rate = 0.1
weight_decay = 0.1
epsilon = 1e-08
bias_first = 1.0 - 0.9**20
bias_second = 1.0 - 0.95**20

HALVES, RING, CORES = 2, 4, 2
PIECES = 4
SMEM = pl.BlockSpec(memory_space=pltpu.SMEM)
VMEM = pl.BlockSpec(memory_space=pltpu.VMEM)
PARAMS = pltpu.CompilerParams(vmem_limit_bytes=62 * 2**20)
FINISH = pltpu.CompilerParams(vmem_limit_bytes=60 * 2**20)
SMALL = pltpu.CompilerParams(vmem_limit_bytes=24 * 2**20)


def cost(flops, size):
    return pl.CostEstimate(flops=flops, bytes_accessed=size, transcendentals=0)


def whole(*shape):
    return pl.BlockSpec(shape, lambda *_: (0,) * len(shape))


def contract_first(left, right):
    return lax.dot_general(
        left, right, (((0,), (0,)), ((), ())), preferred_element_type=jnp.float32
    )


def permutation(half_step, ring_step, core_step):
    pairs = []
    for half in range(HALVES):
        for ring in range(RING):
            for core in range(CORES):
                source = (half * RING + ring) * CORES + core
                target = (half ^ half_step) * RING + (ring + ring_step) % RING
                pairs.append((source, target * CORES + (core ^ core_step)))
    return pairs


def pack_kernel(place_ref, rows_ref, grad_ref, master_ref, first_ref, second_ref, *outs):
    table, columns = grad_ref.shape
    tokens = rows_ref.shape[1]
    rows = master_ref.shape[1]
    owners = HALVES * RING * CORES // PIECES
    width = columns // owners
    onehot = (
        (lax.broadcasted_iota(jnp.int32, (table, tokens), 0) == rows_ref[...])
        .astype(jnp.float32)
        .astype(jnp.bfloat16)
    )
    selected = contract_first(onehot, grad_ref[...]).astype(jnp.bfloat16)
    ring = place_ref[1]
    for here in range(RING):
        for piece in range(PIECES):

            @pl.when((ring == here) & (pl.program_id(0) == piece))
            def _(here=here, piece=piece):
                for local in range(owners):
                    owner = piece * owners + local
                    half, place = owner // (RING * CORES), owner // CORES % RING
                    out = outs[(place - here) % RING]
                    take = pl.ds(local * width, width)
                    put = pl.ds((owner % CORES * HALVES + half) * width, width)
                    out[0:tokens, put] = selected[:, local * width : (local + 1) * width]
                    at = tokens
                    out[at : at + rows, put] = master_ref[0, :, take].astype(jnp.bfloat16)
                    out[at + rows : at + 2 * rows, put] = first_ref[0, :, take]
                    out[at + 2 * rows : at + 3 * rows, put] = second_ref[0, :, take]


def pack(place, train_rows, out_grad, master, moment1, moment2):
    tokens = train_rows.shape[1]
    rows = master.shape[1]
    table, columns = out_grad.shape
    shape = (tokens + 3 * rows, columns // RING)
    state = pl.BlockSpec((1, rows, columns // PIECES), lambda i: (0, 0, i))
    return pl.pallas_call(
        pack_kernel,
        grid=(PIECES,),
        out_shape=[jax.ShapeDtypeStruct(shape, jnp.bfloat16)] * RING,
        in_specs=[
            SMEM,
            whole(1, tokens),
            pl.BlockSpec((table, columns // PIECES), lambda i: (0, i)),
            state,
            state,
            state,
        ],
        out_specs=[whole(*shape)] * RING,
        compiler_params=PARAMS,
        cost_estimate=cost(2 * tokens * out_grad.size, 7_000_000),
    )(place, train_rows, out_grad, master, moment1, moment2)


def split(flag, values):
    width = values.shape[-1] // 2
    low, high = values[..., :width], values[..., width:]
    return jnp.where(flag == 0, low, high), jnp.where(flag == 0, high, low)


def core_kernel(place_ref, *refs):
    parts, (mine_ref, theirs_ref) = refs[:RING], refs[RING:]
    ring, core = place_ref[1], place_ref[2]
    for step in range(RING):
        mine, theirs = split(core, parts[step][...])
        source = (ring - step + RING) % RING
        mine_ref[source] = mine
        theirs_ref[source] = theirs


def split_cores(place, parts):
    rows, width = parts[0].shape
    block = rows // 2
    return pl.pallas_call(
        core_kernel,
        grid=(rows // block,),
        out_shape=[jax.ShapeDtypeStruct((RING, rows, width // 2), jnp.bfloat16)] * 2,
        in_specs=[SMEM] + [pl.BlockSpec((block, width), lambda i: (i, 0))] * RING,
        out_specs=[pl.BlockSpec((RING, block, width // 2), lambda i: (0, i, 0))] * 2,
        compiler_params=PARAMS,
        cost_estimate=cost(0, 5_000_000),
    )(place, *parts)


def gradient_kernel(place_ref, acts_ref, mine_ref, near_ref, out_ref):
    core = place_ref[2]
    total = None
    for ring in range(RING):
        left = jnp.concatenate(
            [acts_ref[ring * CORES + core], acts_ref[ring * CORES + 1 - core]], axis=0
        )
        right = jnp.concatenate([mine_ref[ring], near_ref[ring]], axis=0)
        product = contract_first(left, right)
        total = product if total is None else total + product
    out_ref[...] = total.astype(out_ref.dtype).reshape(out_ref.shape)


def gradient_rows(place, acts, mine, near, tokens, other_half, dtype):
    group_tokens, units = acts.shape
    sources = RING * CORES
    blocks = 2
    block = units // HALVES // blocks
    width = mine.shape[2]
    rows = units // HALVES // sources
    operand = pl.BlockSpec((RING, tokens, width), lambda i, place: (0, 0, 0))
    return pl.pallas_call(
        gradient_kernel,
        out_shape=jax.ShapeDtypeStruct((sources, rows, width), dtype),
        grid_spec=pltpu.PrefetchScalarGridSpec(
            num_scalar_prefetch=1,
            grid=(blocks,),
            in_specs=[
                pl.BlockSpec(
                    (sources, tokens, block),
                    lambda i, place: (
                        0,
                        0,
                        jnp.bitwise_xor(place[0], other_half) * blocks + i,
                    ),
                ),
                operand,
                operand,
            ],
            out_specs=pl.BlockSpec(
                (sources // blocks, rows, width), lambda i, place: (i, 0, 0)
            ),
        ),
        compiler_params=PARAMS,
        cost_estimate=cost(2 * block * blocks * width * group_tokens, 4_000_000),
    )(place, acts.reshape(sources, tokens, units), mine, near)


def finish_kernel(
    tokens, place_ref, kept_ref, far_ref, mine_ref, near_ref, hidden_ref, own_ref, cross_ref, sums
):
    rows = kept_ref.shape[1]
    total = None
    for step, states in enumerate((mine_ref, near_ref)):
        core = jnp.bitwise_xor(place_ref[2], step)
        gradient = kept_ref[core] + far_ref[core].astype(jnp.float32)
        master, first_old, second_old = (
            states[0, tokens + k * rows : tokens + (k + 1) * rows, :].astype(jnp.float32)
            for k in range(3)
        )
        first = beta_one * first_old + (1.0 - beta_one) * gradient
        second = beta_two * second_old + (1.0 - beta_two) * gradient * gradient
        update = first / bias_first / (jnp.sqrt(second / bias_second) + epsilon)
        tile = (master * (1.0 - learn_rate * weight_decay) - learn_rate * update).astype(
            jnp.bfloat16
        )
        product = contract_first(hidden_ref[core], tile)
        total = product if total is None else total + product

    @pl.when(pl.program_id(0) == 0)
    def _():
        sums[...] = total

    @pl.when(pl.program_id(0) > 0)
    def _():
        sums[...] += total

    @pl.when(pl.program_id(0) == RING - 1)
    def _():
        own, cross = split(place_ref[0], sums[...])
        own_ref[...] = own.reshape(own_ref.shape)
        cross_ref[...] = cross.astype(jnp.bfloat16).reshape(cross_ref.shape)


def finish(tokens, place, kept, far, mine, near, hidden):
    _, rows, width = kept.shape
    slots = hidden.shape[2]
    shape = (2, slots // 2, width // 2)
    pair = pl.BlockSpec((CORES, rows, width), lambda i: (i, 0, 0))
    states = pl.BlockSpec((1, mine.shape[1], width), lambda i: (i, 0, 0))
    return pl.pallas_call(
        functools.partial(finish_kernel, tokens),
        grid=(RING,),
        out_shape=[
            jax.ShapeDtypeStruct(shape, jnp.float32),
            jax.ShapeDtypeStruct(shape, jnp.bfloat16),
        ],
        in_specs=[
            SMEM,
            pair,
            pair,
            states,
            states,
            pl.BlockSpec((CORES, rows, slots), lambda i: (i, 0, 0)),
        ],
        out_specs=[whole(*shape)] * 2,
        scratch_shapes=[pltpu.VMEM((slots, width), jnp.float32)],
        compiler_params=FINISH,
        cost_estimate=cost(20 * kept.size, 5_000_000),
    )(place, kept, far, mine, near, hidden)


def turn_kernel(mixed_ref, out_ref):
    gates, slots, units = mixed_ref.shape
    width = out_ref.shape[2]
    for gate in range(gates):
        for pair in range(units // (2 * width)):
            turned = mixed_ref[gate, :, pair * 2 * width : (pair + 1) * 2 * width].T
            turned = turned.astype(jnp.bfloat16)
            out_ref[2 * pair, gate] = turned[:width]
            out_ref[2 * pair + 1, gate] = turned[width:]


def turn(mixed, shards):
    gates, slots, units = mixed.shape
    return pl.pallas_call(
        turn_kernel,
        out_shape=jax.ShapeDtypeStruct((shards, gates, units // shards, slots), jnp.bfloat16),
        in_specs=[VMEM],
        out_specs=VMEM,
        compiler_params=SMALL,
        cost_estimate=cost(0, 1_500_000),
    )(mixed)


def hidden_kernel(shares_ref, out_ref):
    sums = jnp.sum(shares_ref[...].astype(jnp.float32), axis=0)
    hidden = (jax.nn.silu(sums[0]) * sums[1]).astype(jnp.bfloat16)
    for shard in range(out_ref.shape[0]):
        out_ref[shard] = hidden


def hidden_units(shares, copies):
    _, _, units, slots = shares.shape
    return pl.pallas_call(
        hidden_kernel,
        out_shape=jax.ShapeDtypeStruct((copies, units, slots), jnp.bfloat16),
        in_specs=[VMEM],
        out_specs=VMEM,
        compiler_params=SMALL,
        cost_estimate=cost(shares.size, 800_000),
    )(shares)


def body(
    hidden_acts,
    train_rows,
    out_grad,
    master,
    moment1,
    moment2,
    gate_up,
    dec_tokens,
    route_ids,
    route_gates,
):
    index = lax.axis_index("dp")
    shards = lax.axis_size("dp")
    half, ring, core = index >> 3, (index >> 1) & (RING - 1), index & (CORES - 1)
    place = jnp.stack([half, ring, core]).astype(jnp.int32)
    token_count, width = dec_tokens.shape
    tokens = train_rows.shape[1]

    sides = [[h * RING * CORES + k for k in range(RING * CORES)] for h in range(HALVES)]
    acts = lax.all_gather(hidden_acts[0], "dp", axis=0, tiled=True, axis_index_groups=sides)
    sends = pack(place, train_rows, out_grad, master, moment1, moment2)
    parts = [sends[0]] + [
        lax.ppermute(sends[step], "dp", permutation(0, step, 0)) for step in range(1, RING)
    ]

    choices_per = route_ids.shape[1]
    expert_count = lax.axis_size("exp")
    capacity = min(token_count, max(2, 2 * choices_per * token_count // expert_count))
    slot_count = expert_count * capacity
    flat_ids = route_ids.reshape(-1)
    onehot = (flat_ids[:, None] == jnp.arange(expert_count, dtype=jnp.int32)[None, :]).astype(
        jnp.int32
    )
    earlier = jnp.cumsum(onehot, axis=0) - onehot
    position = jnp.sum(earlier * onehot, axis=1)
    slot_index = flat_ids * capacity + position
    placement = (slot_index[:, None] == jnp.arange(slot_count, dtype=jnp.int32)[None, :]).astype(
        jnp.bfloat16
    )
    repeated = jnp.repeat(dec_tokens, choices_per, axis=0)
    outgoing = jnp.einsum(
        "rs,rd->sd", placement, repeated, preferred_element_type=jnp.float32
    ).astype(jnp.bfloat16)
    arrived = lax.all_to_all(
        outgoing.reshape(expert_count, capacity, width),
        "exp",
        split_axis=0,
        concat_axis=0,
        tiled=True,
    )
    arrived, held = lax.optimization_barrier((arrived, parts))
    rows_in = arrived.reshape(slot_count, width)

    mixed = jnp.einsum(
        "dgf,sd->gsf", gate_up[0], rows_in, preferred_element_type=jnp.float32
    )
    shares = lax.all_to_all(
        turn(mixed, shards), "dp", split_axis=0, concat_axis=0, tiled=True
    )
    hidden = lax.all_to_all(
        hidden_units(shares, RING * CORES),
        "dp",
        split_axis=0,
        concat_axis=0,
        tiled=True,
        axis_index_groups=sides,
    )

    across_cores, across_halves = permutation(0, 0, 1), permutation(1, 0, 0)
    mine, theirs = split_cores(place, held)
    near = lax.ppermute(theirs, "dp", across_cores)
    cross = gradient_rows(place, acts, mine, near, tokens, 1, jnp.bfloat16)
    far = lax.ppermute(cross, "dp", across_halves)
    kept = gradient_rows(place, acts, mine, near, tokens, 0, jnp.float32)
    kept_results, cross_results = finish(tokens, place, kept, far, mine, near, hidden)
    far_results = lax.ppermute(cross_results, "dp", across_halves)
    results = (kept_results + far_results.astype(jnp.float32)).astype(jnp.bfloat16)
    returned = lax.all_to_all(
        results.reshape(expert_count, capacity, width),
        "exp",
        split_axis=0,
        concat_axis=0,
        tiled=True,
    )
    back_rows = returned.reshape(slot_count, width)
    chosen = jnp.einsum("rs,sd->rd", placement, back_rows, preferred_element_type=jnp.float32)
    weighted = chosen.reshape(token_count, choices_per, width) * route_gates[:, :, None]
    return jnp.sum(weighted, axis=1).astype(jnp.bfloat16)


def solution(mesh):
    in_specs = (
        P("exp", "dp", None),
        P("exp", "dp"),
        P("dp", None),
        P("exp", "dp", None),
        P("exp", "dp", None),
        P("exp", "dp", None),
        P("exp", "dp", None, None),
        P("exp", "dp"),
        P("exp", None),
        P("exp", None),
    )
    out_specs = P("exp", "dp")
    return jax.shard_map(body, mesh=mesh, in_specs=in_specs, out_specs=out_specs, check_vma=False)
```

```python
import functools

import jax
import jax.numpy as jnp
from jax import lax
from jax.experimental import pallas as pl
from jax.experimental.pallas import tpu as pltpu
from jax.sharding import PartitionSpec as P

beta_one = 0.9
beta_two = 0.95
learn_rate = 0.1
weight_decay = 0.1
epsilon = 1e-08
bias_first = 1.0 - 0.9**20
bias_second = 1.0 - 0.95**20

HALVES, RING, CORES = 2, 4, 2
PIECES = 2
SMEM = pl.BlockSpec(memory_space=pltpu.SMEM)
VMEM = pl.BlockSpec(memory_space=pltpu.VMEM)
PARAMS = pltpu.CompilerParams(vmem_limit_bytes=62 * 2**20)
FINISH = pltpu.CompilerParams(vmem_limit_bytes=60 * 2**20)
SMALL = pltpu.CompilerParams(vmem_limit_bytes=24 * 2**20)


def cost(flops, size):
    return pl.CostEstimate(flops=flops, bytes_accessed=size, transcendentals=0)


def whole(*shape):
    return pl.BlockSpec(shape, lambda *_: (0,) * len(shape))


def contract_first(left, right):
    return lax.dot_general(
        left, right, (((0,), (0,)), ((), ())), preferred_element_type=jnp.float32
    )


def permutation(half_step, ring_step, core_step):
    pairs = []
    for half in range(HALVES):
        for ring in range(RING):
            for core in range(CORES):
                source = (half * RING + ring) * CORES + core
                target = (half ^ half_step) * RING + (ring + ring_step) % RING
                pairs.append((source, target * CORES + (core ^ core_step)))
    return pairs


def pack_kernel(rows_ref, grad_ref, master_ref, first_ref, second_ref, *outs):
    table, columns = grad_ref.shape
    tokens = rows_ref.shape[1]
    rows = master_ref.shape[1]
    owners = HALVES * RING * CORES // PIECES
    width = columns // owners
    onehot = (
        (lax.broadcasted_iota(jnp.int32, (table, tokens), 0) == rows_ref[...])
        .astype(jnp.float32)
        .astype(jnp.bfloat16)
    )
    selected = contract_first(onehot, grad_ref[...]).astype(jnp.bfloat16)
    ring = lax.axis_index("dp") // CORES % RING
    for here in range(RING):
        for piece in range(PIECES):

            @pl.when((ring == here) & (pl.program_id(0) == piece))
            def _(here=here, piece=piece):
                for local in range(owners):
                    owner = piece * owners + local
                    half, place = owner // (RING * CORES), owner // CORES % RING
                    out = outs[(place - here) % RING]
                    take = pl.ds(local * width, width)
                    put = pl.ds((owner % CORES * HALVES + half) * width, width)
                    out[0:tokens, put] = selected[:, local * width : (local + 1) * width]
                    at = tokens
                    out[at : at + rows, put] = master_ref[0, :, take].astype(jnp.bfloat16)
                    out[at + rows : at + 2 * rows, put] = first_ref[0, :, take]
                    out[at + 2 * rows : at + 3 * rows, put] = second_ref[0, :, take]


def pack(train_rows, out_grad, master, moment1, moment2):
    tokens = train_rows.shape[1]
    rows = master.shape[1]
    table, columns = out_grad.shape
    shape = (tokens + 3 * rows, columns // RING)
    state = pl.BlockSpec((1, rows, columns // PIECES), lambda i: (0, 0, i))
    return pl.pallas_call(
        pack_kernel,
        grid=(PIECES,),
        out_shape=[jax.ShapeDtypeStruct(shape, jnp.bfloat16)] * RING,
        in_specs=[
            whole(1, tokens),
            pl.BlockSpec((table, columns // PIECES), lambda i: (0, i)),
            state,
            state,
            state,
        ],
        out_specs=[whole(*shape)] * RING,
        compiler_params=PARAMS,
        cost_estimate=cost(2 * tokens * out_grad.size, 7_000_000),
    )(train_rows, out_grad, master, moment1, moment2)


def split(flag, values):
    width = values.shape[-1] // 2
    low, high = values[..., :width], values[..., width:]
    return jnp.where(flag == 0, low, high), jnp.where(flag == 0, high, low)


def core_kernel(place_ref, *refs):
    parts, (mine_ref, theirs_ref) = refs[:RING], refs[RING:]
    ring, core = place_ref[1], place_ref[2]
    for step in range(RING):
        mine, theirs = split(core, parts[step][...])
        source = (ring - step + RING) % RING
        mine_ref[source] = mine
        theirs_ref[source] = theirs


def split_cores(place, parts):
    rows, width = parts[0].shape
    block = rows // 2
    return pl.pallas_call(
        core_kernel,
        grid=(rows // block,),
        out_shape=[jax.ShapeDtypeStruct((RING, rows, width // 2), jnp.bfloat16)] * 2,
        in_specs=[SMEM] + [pl.BlockSpec((block, width), lambda i: (i, 0))] * RING,
        out_specs=[pl.BlockSpec((RING, block, width // 2), lambda i: (0, i, 0))] * 2,
        compiler_params=PARAMS,
        cost_estimate=cost(0, 5_000_000),
    )(place, *parts)


def gradient_kernel(place_ref, acts_ref, mine_ref, near_ref, out_ref):
    core = place_ref[2]
    total = None
    for ring in range(RING):
        left = jnp.concatenate(
            [acts_ref[ring * CORES + core], acts_ref[ring * CORES + 1 - core]], axis=0
        )
        right = jnp.concatenate([mine_ref[ring], near_ref[ring]], axis=0)
        product = contract_first(left, right)
        total = product if total is None else total + product
    out_ref[...] = total.astype(out_ref.dtype).reshape(out_ref.shape)


def gradient_rows(place, acts, mine, near, tokens, other_half, dtype):
    group_tokens, units = acts.shape
    sources = RING * CORES
    blocks = 2
    block = units // HALVES // blocks
    width = mine.shape[2]
    rows = units // HALVES // sources
    operand = pl.BlockSpec((RING, tokens, width), lambda i, place: (0, 0, 0))
    return pl.pallas_call(
        gradient_kernel,
        out_shape=jax.ShapeDtypeStruct((sources, rows, width), dtype),
        grid_spec=pltpu.PrefetchScalarGridSpec(
            num_scalar_prefetch=1,
            grid=(blocks,),
            in_specs=[
                pl.BlockSpec(
                    (sources, tokens, block),
                    lambda i, place: (
                        0,
                        0,
                        jnp.bitwise_xor(place[0], other_half) * blocks + i,
                    ),
                ),
                operand,
                operand,
            ],
            out_specs=pl.BlockSpec(
                (sources // blocks, rows, width), lambda i, place: (i, 0, 0)
            ),
        ),
        compiler_params=PARAMS,
        cost_estimate=cost(2 * block * blocks * width * group_tokens, 4_000_000),
    )(place, acts.reshape(sources, tokens, units), mine, near)


def finish_kernel(
    tokens, place_ref, kept_ref, far_ref, mine_ref, near_ref, hidden_ref, own_ref, cross_ref, sums
):
    rows = kept_ref.shape[1]
    total = None
    for step, states in enumerate((mine_ref, near_ref)):
        core = jnp.bitwise_xor(place_ref[2], step)
        gradient = kept_ref[core] + far_ref[core].astype(jnp.float32)
        master, first_old, second_old = (
            states[0, tokens + k * rows : tokens + (k + 1) * rows, :].astype(jnp.float32)
            for k in range(3)
        )
        first = beta_one * first_old + (1.0 - beta_one) * gradient
        second = beta_two * second_old + (1.0 - beta_two) * gradient * gradient
        update = first / bias_first / (jnp.sqrt(second / bias_second) + epsilon)
        tile = (master * (1.0 - learn_rate * weight_decay) - learn_rate * update).astype(
            jnp.bfloat16
        )
        product = contract_first(hidden_ref[core], tile)
        total = product if total is None else total + product

    @pl.when(pl.program_id(0) == 0)
    def _():
        sums[...] = total

    @pl.when(pl.program_id(0) > 0)
    def _():
        sums[...] += total

    @pl.when(pl.program_id(0) == RING - 1)
    def _():
        own, cross = split(place_ref[0], sums[...])
        own_ref[...] = own.reshape(own_ref.shape)
        cross_ref[...] = cross.astype(jnp.bfloat16).reshape(cross_ref.shape)


def finish(tokens, place, kept, far, mine, near, hidden):
    _, rows, width = kept.shape
    slots = hidden.shape[2]
    shape = (2, slots // 2, width // 2)
    pair = pl.BlockSpec((CORES, rows, width), lambda i: (i, 0, 0))
    states = pl.BlockSpec((1, mine.shape[1], width), lambda i: (i, 0, 0))
    return pl.pallas_call(
        functools.partial(finish_kernel, tokens),
        grid=(RING,),
        out_shape=[
            jax.ShapeDtypeStruct(shape, jnp.float32),
            jax.ShapeDtypeStruct(shape, jnp.bfloat16),
        ],
        in_specs=[
            SMEM,
            pair,
            pair,
            states,
            states,
            pl.BlockSpec((CORES, rows, slots), lambda i: (i, 0, 0)),
        ],
        out_specs=[whole(*shape)] * 2,
        scratch_shapes=[pltpu.VMEM((slots, width), jnp.float32)],
        compiler_params=FINISH,
        cost_estimate=cost(20 * kept.size, 5_000_000),
    )(place, kept, far, mine, near, hidden)


def turn_kernel(mixed_ref, out_ref):
    gates, slots, units = mixed_ref.shape
    width = out_ref.shape[2]
    for gate in range(gates):
        for pair in range(units // (2 * width)):
            turned = mixed_ref[gate, :, pair * 2 * width : (pair + 1) * 2 * width].T
            turned = turned.astype(jnp.bfloat16)
            out_ref[2 * pair, gate] = turned[:width]
            out_ref[2 * pair + 1, gate] = turned[width:]


def turn(mixed, shards):
    gates, slots, units = mixed.shape
    return pl.pallas_call(
        turn_kernel,
        out_shape=jax.ShapeDtypeStruct((shards, gates, units // shards, slots), jnp.bfloat16),
        in_specs=[VMEM],
        out_specs=VMEM,
        compiler_params=SMALL,
        cost_estimate=cost(0, 1_500_000),
    )(mixed)


def hidden_kernel(shares_ref, out_ref):
    sums = jnp.sum(shares_ref[...].astype(jnp.float32), axis=0)
    hidden = (jax.nn.silu(sums[0]) * sums[1]).astype(jnp.bfloat16)
    for shard in range(out_ref.shape[0]):
        out_ref[shard] = hidden


def hidden_units(shares, copies):
    _, _, units, slots = shares.shape
    return pl.pallas_call(
        hidden_kernel,
        out_shape=jax.ShapeDtypeStruct((copies, units, slots), jnp.bfloat16),
        in_specs=[VMEM],
        out_specs=VMEM,
        compiler_params=SMALL,
        cost_estimate=cost(shares.size, 800_000),
    )(shares)


def body(
    hidden_acts,
    train_rows,
    out_grad,
    master,
    moment1,
    moment2,
    gate_up,
    dec_tokens,
    route_ids,
    route_gates,
):
    index = lax.axis_index("dp")
    shards = lax.axis_size("dp")
    half, ring, core = index >> 3, (index >> 1) & (RING - 1), index & (CORES - 1)
    place = jnp.stack([half, ring, core]).astype(jnp.int32)
    token_count, width = dec_tokens.shape
    tokens = train_rows.shape[1]

    sides = [[h * RING * CORES + k for k in range(RING * CORES)] for h in range(HALVES)]
    acts = lax.all_gather(hidden_acts[0], "dp", axis=0, tiled=True, axis_index_groups=sides)
    sends = pack(train_rows, out_grad, master, moment1, moment2)
    parts = [sends[0]] + [
        lax.ppermute(sends[step], "dp", permutation(0, step, 0)) for step in range(1, RING)
    ]

    choices_per = route_ids.shape[1]
    expert_count = lax.axis_size("exp")
    capacity = min(token_count, max(2, 2 * choices_per * token_count // expert_count))
    slot_count = expert_count * capacity
    flat_ids = route_ids.reshape(-1)
    onehot = (flat_ids[:, None] == jnp.arange(expert_count, dtype=jnp.int32)[None, :]).astype(
        jnp.int32
    )
    earlier = jnp.cumsum(onehot, axis=0) - onehot
    position = jnp.sum(earlier * onehot, axis=1)
    slot_index = flat_ids * capacity + position
    placement = (slot_index[:, None] == jnp.arange(slot_count, dtype=jnp.int32)[None, :]).astype(
        jnp.bfloat16
    )
    repeated = jnp.repeat(dec_tokens, choices_per, axis=0)
    outgoing = jnp.einsum(
        "rs,rd->sd", placement, repeated, preferred_element_type=jnp.float32
    ).astype(jnp.bfloat16)
    arrived = lax.all_to_all(
        outgoing.reshape(expert_count, capacity, width),
        "exp",
        split_axis=0,
        concat_axis=0,
        tiled=True,
    )
    arrived, held = lax.optimization_barrier((arrived, parts))
    rows_in = arrived.reshape(slot_count, width)

    mixed = jnp.einsum(
        "dgf,sd->gsf", gate_up[0], rows_in, preferred_element_type=jnp.float32
    )
    shares = lax.all_to_all(
        turn(mixed, shards), "dp", split_axis=0, concat_axis=0, tiled=True
    )
    hidden = lax.all_to_all(
        hidden_units(shares, RING * CORES),
        "dp",
        split_axis=0,
        concat_axis=0,
        tiled=True,
        axis_index_groups=sides,
    )

    across_cores, across_halves = permutation(0, 0, 1), permutation(1, 0, 0)
    mine, theirs = split_cores(place, held)
    near = lax.ppermute(theirs, "dp", across_cores)
    cross = gradient_rows(place, acts, mine, near, tokens, 1, jnp.bfloat16)
    far = lax.ppermute(cross, "dp", across_halves)
    kept = gradient_rows(place, acts, mine, near, tokens, 0, jnp.float32)
    kept_results, cross_results = finish(tokens, place, kept, far, mine, near, hidden)
    far_results = lax.ppermute(cross_results, "dp", across_halves)
    results = (kept_results + far_results.astype(jnp.float32)).astype(jnp.bfloat16)
    returned = lax.all_to_all(
        results.reshape(expert_count, capacity, width),
        "exp",
        split_axis=0,
        concat_axis=0,
        tiled=True,
    )
    back_rows = returned.reshape(slot_count, width)
    chosen = jnp.einsum("rs,sd->rd", placement, back_rows, preferred_element_type=jnp.float32)
    weighted = chosen.reshape(token_count, choices_per, width) * route_gates[:, :, None]
    return jnp.sum(weighted, axis=1).astype(jnp.bfloat16)


def solution(mesh):
    in_specs = (
        P("exp", "dp", None),
        P("exp", "dp"),
        P("dp", None),
        P("exp", "dp", None),
        P("exp", "dp", None),
        P("exp", "dp", None),
        P("exp", "dp", None, None),
        P("exp", "dp"),
        P("exp", None),
        P("exp", None),
    )
    out_specs = P("exp", "dp")
    return jax.shard_map(body, mesh=mesh, in_specs=in_specs, out_specs=out_specs, check_vma=False)
```
